32 devices in a mesh: member: 16 (over z, y, x), row: 2 (over core).
Axes of the slice: x: 2, y: 2, z: 4, core: 2. Of those that a mesh axis runs over, the one named last changes fastest.
Arguments:
- fields: float32 [32, 3, 32, 1024], P('member', None, 'row'), may hold values from -1.5 to 1.5
- bathymetry: int32 [32, 1024], P('row'), may hold values from 250 to 300
- copy_lists: int32 [3, 5, 32], replicated, may hold values from 0 to 31, as said below
Outputs:
- final_fields: float32 [32, 3, 32, 1024], P('member', None, 'row')
The draws below stay inside these ranges and needn't reach their ends.
Inputs may be any that keep to these rules, and one draw needn't show every extreme that they name: copy_lists[c, s, m] is m or m xor 2 to the power s; members m and m xor 2 to the power s either both keep their own state or both take the same one of the two.
All inputs are finite; a program needn't handle non-finite values.
Results may differ from the reference program's by a relative error of at most 0.00002.
Values sent between devices are 32-bit elements; how exact they have to be, the bound alone decides.
A program may use at most 64 MiB of HBM per device.

```python
import jax
import jax.numpy as jnp

NX = 1024
STEPS = 4
CYCLES = 3
NY = 32
MEMBERS = 32
SECTIONS = 5


def draw_copy_lists(key, part):
    outcome = jax.random.randint(key, (CYCLES, SECTIONS, MEMBERS), 0, 3).astype(jnp.int32)
    members = jnp.arange(MEMBERS, dtype=jnp.int32)
    powers = (2 ** jnp.arange(SECTIONS, dtype=jnp.int32))[None, :, None]
    partner = jnp.bitwise_xor(members[None, None, :], powers)
    lower = jnp.minimum(members[None, None, :], partner)
    upper = jnp.maximum(members[None, None, :], partner)
    lower_full = jnp.broadcast_to(lower, (CYCLES, SECTIONS, MEMBERS)).astype(jnp.int32)
    pair_kind = jnp.take_along_axis(outcome, lower_full, axis=2)
    keep = jnp.broadcast_to(members[None, None, :], (CYCLES, SECTIONS, MEMBERS))
    sources = jnp.where(pair_kind == 0, keep, jnp.where(pair_kind == 1, lower_full, upper))
    return sources.astype(jnp.int32)


def with_ends(result, key, low, high):
    shape = result.shape
    place = [jax.random.randint(jax.random.fold_in(key, axis), (), 0, shape[axis]) for axis in range(len(shape))]
    result = result.at[tuple(place)].set(low)
    longest = shape.index(max(shape))
    place[longest] = (place[longest] + 1) % shape[longest]
    return result.at[tuple(place)].set(high)


def steps_of(key, shape, cuts, smallest, high):
    def one(position, parts):
        draws = jax.random.uniform(jax.random.fold_in(jax.random.fold_in(key, 6), position), (parts,), jnp.float32, smallest / len(cuts), high / len(cuts))
        return jnp.repeat(jnp.exp(draws), shape[position] // parts).reshape((-1,) + (1,) * (len(shape) - position - 1))

    loudness = one(*cuts[0])
    for cut in cuts[1:]:
        loudness = loudness * one(*cut)
    return loudness


def centred(stream_key, shape, width, limit, pieces=(), kind=jnp.bfloat16):
    result = width * jax.random.normal(stream_key, shape, jnp.float32)
    if pieces:
        result = result * steps_of(stream_key, shape, pieces, -0.22, 0.18)
    return jnp.clip(result, -limit, limit).astype(kind)


def setup_inputs(seed: int = 0) -> dict:
    keys = jax.random.split(jax.random.key(seed), 4)
    return {
        "fields": centred(keys[0], (MEMBERS, 3, NY, NX), 0.3, 1.5, ((0, 16), (2, 2)), jnp.float32),
        "bathymetry": with_ends(jax.random.randint(keys[1], (NY, NX), 250, 301), jax.random.fold_in(keys[1], 1), 250, 300).astype(jnp.int32),
        "copy_lists": draw_copy_lists(jax.random.fold_in(keys[3], 71), 0),
    }


gravity = 2.0
coriolis = 0.1
friction = 0.02
time_step = 0.25


def rates(padded, depth_pad):
    height = padded[:, 0]
    east = padded[:, 1]
    north = padded[:, 2]
    column = depth_pad + height
    flux_x = column * east
    flux_y = column * north
    diff_x = (jnp.roll(flux_x, -1, -1) - jnp.roll(flux_x, 1, -1))[:, 1:-1]
    diff_y = flux_y[:, 2:] - flux_y[:, :-2]
    rate_h = -0.5 * (diff_x + diff_y)
    slope_x = (jnp.roll(height, -1, -1) - jnp.roll(height, 1, -1))[:, 1:-1]
    slope_y = height[:, 2:] - height[:, :-2]
    east_mid = east[:, 1:-1]
    north_mid = north[:, 1:-1]
    rate_u = -0.5 * gravity * slope_x + coriolis * north_mid - friction * east_mid
    rate_v = -0.5 * gravity * slope_y - coriolis * east_mid - friction * north_mid
    return jnp.stack([rate_h, rate_u, rate_v], 1)


def wrap_rows(field):
    return jnp.concatenate([field[..., -1:, :], field, field[..., :1, :]], axis=-2)


def reference(fields, bathymetry, copy_lists):
    depth = bathymetry.astype(jnp.float32) / 100.0
    depth_pad = wrap_rows(depth)
    current = fields
    for cycle_no in range(CYCLES):
        for step_no in range(STEPS):
            first_rate = rates(wrap_rows(current), depth_pad)
            middle = current + time_step * first_rate
            second_rate = rates(wrap_rows(middle), depth_pad)
            current = current + (0.5 * time_step) * (first_rate + second_rate)
        for section_no in range(SECTIONS):
            current = jnp.take(current, copy_lists[cycle_no, section_no], axis=0)
    return current
```

```python
import functools

import jax
import jax.numpy as jnp
from jax import lax
from jax.experimental import pallas as pl
from jax.experimental.pallas import tpu as pltpu
from jax.sharding import PartitionSpec as P

STEPS = 4
CYCLES = 3


gravity = 2.0
coriolis = 0.1
friction = 0.02
time_step = 0.25

LANES = 128
SUBLANES = 8
MESH = pl.DeviceIdType.MESH


def extended(x, sides, width):
    for axis, dim in sides:
        devices, length = (lax.axis_size(axis), x.shape[dim])
        up = [(i, (i + 1) % devices) for i in range(devices)]
        down = [(j, i) for i, j in up]
        last = lax.slice_in_dim(x, length - width, length, axis=dim)
        leading = lax.slice_in_dim(x, 0, width, axis=dim)
        before = lax.ppermute(last, axis, up)
        after = lax.ppermute(leading, axis, down)
        x = jnp.concatenate([before, x, after], axis=dim)
    return x


def rates(padded, depth_pad):
    height = padded[:, 0]
    east = padded[:, 1]
    north = padded[:, 2]
    column = depth_pad + height
    flux_x = column * east
    flux_y = column * north
    diff_x = (jnp.roll(flux_x, -1, -1) - jnp.roll(flux_x, 1, -1))[:, 1:-1]
    diff_y = flux_y[:, 2:] - flux_y[:, :-2]
    rate_h = -0.5 * (diff_x + diff_y)
    slope_x = (jnp.roll(height, -1, -1) - jnp.roll(height, 1, -1))[:, 1:-1]
    slope_y = height[:, 2:] - height[:, :-2]
    east_mid = east[:, 1:-1]
    north_mid = north[:, 1:-1]
    rate_u = -0.5 * gravity * slope_x + coriolis * north_mid - friction * east_mid
    rate_v = -0.5 * gravity * slope_y - coriolis * east_mid - friction * north_mid
    return jnp.stack([rate_h, rate_u, rate_v], 1)


def trim_depth(depth_full, width):
    offset = 2 * STEPS - width
    total = depth_full.shape[0]
    return depth_full[offset : total - offset]


def general_body(fields, bathymetry, copy_lists):
    depth_ext = extended(bathymetry, (("row", 0),), 2 * STEPS)
    depth_full = depth_ext.astype(jnp.float32) / 100.0
    current = fields
    for _ in range(CYCLES):
        padded = extended(current, (("row", 2),), 2 * STEPS)
        for step_no in range(STEPS):
            width = 2 * (STEPS - step_no)
            first_rate = rates(padded, trim_depth(depth_full, width))
            rows_now = padded.shape[2]
            middle = padded[:, :, 1 : rows_now - 1] + time_step * first_rate
            second_rate = rates(middle, trim_depth(depth_full, width - 1))
            rows_mid = first_rate.shape[2]
            padded = padded[:, :, 2 : rows_now - 2] + 0.5 * time_step * (
                first_rate[:, :, 1 : rows_mid - 1] + second_rate
            )
        current = padded
    sources = jnp.arange(copy_lists.shape[2], dtype=jnp.int32)
    for cycle_no in reversed(range(copy_lists.shape[0])):
        for section_no in reversed(range(copy_lists.shape[1])):
            sources = jnp.take(copy_lists[cycle_no, section_no], sources)
    spread = lax.all_to_all(current, "member", split_axis=3, concat_axis=0, tiled=True)
    return lax.all_to_all(
        jnp.take(spread, sources, axis=0), "member", split_axis=0, concat_axis=3, tiled=True
    )


def advance(state, flux, depth, target, target_flux, base, scale, col, rows, lane):
    cols = state.shape[2] // LANES
    here = pl.ds(col * LANES, LANES)
    left = pl.ds((col - 1) % cols * LANES, LANES)
    right = pl.ds((col + 1) % cols * LANES, LANES)

    def from_left(ref):
        return pltpu.roll(jnp.where(lane == LANES - 1, ref[:, left], ref[:, here]), 1, 1)

    def from_right(ref):
        return pltpu.roll(jnp.where(lane == 0, ref[:, right], ref[:, here]), LANES - 1, 1)

    height = state[0, :, here]
    east = state[1, :, here]
    north = state[2, :, here]
    rest = depth[:, here]
    flux_y = (rest + height) * north
    diff_x = from_right(flux) - from_left(flux)
    diff_y = pltpu.roll(flux_y, rows - 1, 0) - pltpu.roll(flux_y, 1, 0)
    slope_x = from_right(state.at[0]) - from_left(state.at[0])
    slope_y = pltpu.roll(height, rows - 1, 0) - pltpu.roll(height, 1, 0)
    keep = 1.0 if base is None else 0.5
    drag = keep - scale * friction
    turn = scale * coriolis
    push = 0.5 * gravity * scale
    new_h = (height if base is None else 0.5 * height) - (0.5 * scale) * (diff_x + diff_y)
    new_u = drag * east + turn * north - push * slope_x
    new_v = drag * north - turn * east - push * slope_y
    if base is not None:
        new_h = new_h + 0.5 * base[0, :, here]
        new_u = new_u + 0.5 * base[1, :, here]
        new_v = new_v + 0.5 * base[2, :, here]
    target[0, :, here] = new_h
    target[1, :, here] = new_u
    target[2, :, here] = new_v
    target_flux[:, here] = (rest + new_h) * new_u


def kernel(
    members_axis, rows_axis, fields, bathymetry, lists, out,
    state, middle, flux, flux_mid, resting, depth, held, picked, sources,
    load_sem, swap_send, swap_recv, spread_send, spread_recv, back_send, back_recv,
):
    group, row_no = lax.axis_index("member"), lax.axis_index("row")
    devices = members_axis * rows_axis
    me = group * rows_axis + row_no
    tile_rows, width = fields.shape[2], fields.shape[3]
    rows = tile_rows * rows_axis
    cols = width // LANES
    local = fields.shape[0]
    part = held.shape[2]
    own_rows = pl.ds(pl.multiple_of(row_no * tile_rows, SUBLANES), tile_rows)

    own_fields = pltpu.make_async_copy(fields.at[row_no], state.at[:, own_rows], load_sem.at[0])
    own_depth = pltpu.make_async_copy(bathymetry, resting.at[own_rows], load_sem.at[1])
    own_fields.start()
    own_depth.start()

    barrier = pltpu.get_barrier_semaphore()

    def greet(k, carry):
        other = lax.rem(me + k, devices)
        pl.semaphore_signal(
            barrier, inc=1, device_id=(other // rows_axis, lax.rem(other, rows_axis)),
            device_id_type=MESH,
        )
        return carry

    lax.fori_loop(1, devices, greet, 0)
    pl.semaphore_wait(barrier, devices - 1)

    swaps = []
    for k in range(1, rows_axis):
        other = lax.rem(row_no + k, rows_axis)
        for n, (src, dst) in enumerate(
            ((bathymetry, resting.at[own_rows]), (fields.at[other], state.at[:, own_rows]))
        ):
            copy = pltpu.make_async_remote_copy(
                src_ref=src, dst_ref=dst,
                send_sem=swap_send.at[2 * k + n], recv_sem=swap_recv.at[2 * k + n],
                device_id=(group, other), device_id_type=MESH,
            )
            copy.start()
            swaps.append(copy)
    own_fields.wait()
    own_depth.wait()
    for copy in swaps:
        copy.wait()

    depth[...] = resting[...].astype(jnp.float32) / 100.0
    flux[...] = (depth[...] + state[0]) * state[1]
    lane = lax.broadcasted_iota(jnp.int32, (rows, LANES), 1)

    def step(_, carry):
        for col in range(cols):
            advance(state, flux, depth, middle, flux_mid, None, time_step, col, rows, lane)
        for col in range(cols):
            advance(middle, flux_mid, depth, state, flux, state, 0.5 * time_step, col, rows, lane)
        return carry

    lax.fori_loop(0, STEPS * CYCLES, step, 0)

    def piece(j, r):
        return state.at[
            :,
            pl.ds(pl.multiple_of(r * tile_rows + j // cols * part, SUBLANES), part),
            pl.ds(pl.multiple_of(lax.rem(j, cols) * LANES, LANES), LANES),
        ]

    def spread_copy(k):
        other = lax.rem(me + k, devices)
        j, r = other // rows_axis, lax.rem(other, rows_axis)
        return pltpu.make_async_remote_copy(
            src_ref=piece(j, r), dst_ref=held.at[me],
            send_sem=spread_send.at[k], recv_sem=spread_recv,
            device_id=(j, r), device_id_type=MESH,
        )

    def start_spread(k, carry):
        spread_copy(k).start()
        return carry

    lax.fori_loop(1, devices, start_spread, 0)
    pltpu.make_async_copy(piece(group, row_no), held.at[me], spread_recv).start()

    def compose(m, carry):
        source = m
        for cycle_no in reversed(range(lists.shape[0])):
            for section_no in reversed(range(lists.shape[1])):
                source = lists[cycle_no, section_no, source]
        sources[m] = source
        return carry

    lax.fori_loop(0, held.shape[0], compose, 0)
    pltpu.make_async_copy(held, held, spread_recv).wait()

    for m in range(held.shape[0]):
        picked[m] = held[sources[m]]

    place = out.at[
        :,
        :,
        pl.ds(pl.multiple_of(group // cols * part, SUBLANES), part),
        pl.ds(pl.multiple_of(lax.rem(group, cols) * LANES, LANES), LANES),
    ]

    def back_copy(k):
        other = lax.rem(group + k, members_axis)
        return pltpu.make_async_remote_copy(
            src_ref=picked.at[pl.ds(other * local, local)], dst_ref=place,
            send_sem=back_send.at[k], recv_sem=back_recv,
            device_id=(other, row_no), device_id_type=MESH,
        )

    def start_back(k, carry):
        back_copy(k).start()
        return carry

    lax.fori_loop(1, members_axis, start_back, 0)
    pltpu.make_async_copy(picked.at[pl.ds(group * local, local)], place, back_recv).start()

    def end_spread(k, carry):
        spread_copy(k).wait_send()
        return carry

    lax.fori_loop(1, devices, end_spread, 0)

    def end_back(k, carry):
        back_copy(k).wait_send()
        return carry

    lax.fori_loop(1, members_axis, end_back, 0)
    pltpu.make_async_copy(out, out, back_recv).wait()


def fast_body(members_axis, rows_axis, fields, bathymetry, copy_lists):
    local, kinds, tile_rows, width = fields.shape
    rows = tile_rows * rows_axis
    part = tile_rows // (members_axis // (width // LANES))
    f32 = jnp.float32
    dma = pltpu.SemaphoreType.DMA
    return pl.pallas_call(
        functools.partial(kernel, members_axis, rows_axis),
        out_shape=jax.ShapeDtypeStruct(fields.shape, f32),
        in_specs=[
            pl.BlockSpec(memory_space=pl.ANY),
            pl.BlockSpec(memory_space=pl.ANY),
            pl.BlockSpec(memory_space=pltpu.SMEM),
        ],
        out_specs=pl.BlockSpec(memory_space=pltpu.VMEM),
        scratch_shapes=[
            pltpu.VMEM((kinds, rows, width), f32),
            pltpu.VMEM((kinds, rows, width), f32),
            pltpu.VMEM((rows, width), f32),
            pltpu.VMEM((rows, width), f32),
            pltpu.VMEM((rows, width), jnp.int32),
            pltpu.VMEM((rows, width), f32),
            pltpu.VMEM((members_axis * local, kinds, part, LANES), f32),
            pltpu.VMEM((members_axis * local, kinds, part, LANES), f32),
            pltpu.SMEM((members_axis * local,), jnp.int32),
            dma((2,)),
            dma((2 * rows_axis,)),
            dma((2 * rows_axis,)),
            dma((members_axis * rows_axis,)),
            dma,
            dma((members_axis,)),
            dma,
        ],
        compiler_params=pltpu.CompilerParams(
            collective_id=0, has_side_effects=True, vmem_limit_bytes=32 * 1024 * 1024
        ),
    )(fields, bathymetry, copy_lists)


def solution(mesh):
    members_axis, rows_axis = mesh.shape["member"], mesh.shape["row"]
    placed = (P("member", None, "row", None), P("row", None), P())

    def body(fields, bathymetry, copy_lists):
        local, _, tile_rows, width = fields.shape
        cols = width // LANES
        splits = max(members_axis // cols, 1)
        fits = (
            local == rows_axis
            and width % LANES == 0
            and members_axis % cols == 0
            and tile_rows % (splits * SUBLANES) == 0
        )
        if fits:
            return fast_body(members_axis, rows_axis, fields, bathymetry, copy_lists)
        return general_body(fields, bathymetry, copy_lists)

    return jax.shard_map(
        body, mesh=mesh, in_specs=placed, out_specs=P("member", None, "row", None), check_vma=False
    )
```

```python
import functools

import jax
import jax.numpy as jnp
from jax import lax
from jax.experimental import pallas as pl
from jax.experimental.pallas import tpu as pltpu
from jax.sharding import PartitionSpec as P

STEPS = 4
CYCLES = 3


gravity = 2.0
coriolis = 0.1
friction = 0.02
time_step = 0.25

LANES = 128
SUBLANES = 8
MESH = pl.DeviceIdType.MESH


def extended(x, sides, width):
    for axis, dim in sides:
        devices, length = (lax.axis_size(axis), x.shape[dim])
        up = [(i, (i + 1) % devices) for i in range(devices)]
        down = [(j, i) for i, j in up]
        last = lax.slice_in_dim(x, length - width, length, axis=dim)
        leading = lax.slice_in_dim(x, 0, width, axis=dim)
        before = lax.ppermute(last, axis, up)
        after = lax.ppermute(leading, axis, down)
        x = jnp.concatenate([before, x, after], axis=dim)
    return x


def rates(padded, depth_pad):
    height = padded[:, 0]
    east = padded[:, 1]
    north = padded[:, 2]
    column = depth_pad + height
    flux_x = column * east
    flux_y = column * north
    diff_x = (jnp.roll(flux_x, -1, -1) - jnp.roll(flux_x, 1, -1))[:, 1:-1]
    diff_y = flux_y[:, 2:] - flux_y[:, :-2]
    rate_h = -0.5 * (diff_x + diff_y)
    slope_x = (jnp.roll(height, -1, -1) - jnp.roll(height, 1, -1))[:, 1:-1]
    slope_y = height[:, 2:] - height[:, :-2]
    east_mid = east[:, 1:-1]
    north_mid = north[:, 1:-1]
    rate_u = -0.5 * gravity * slope_x + coriolis * north_mid - friction * east_mid
    rate_v = -0.5 * gravity * slope_y - coriolis * east_mid - friction * north_mid
    return jnp.stack([rate_h, rate_u, rate_v], 1)


def trim_depth(depth_full, width):
    offset = 2 * STEPS - width
    total = depth_full.shape[0]
    return depth_full[offset : total - offset]


def general_body(fields, bathymetry, copy_lists):
    depth_ext = extended(bathymetry, (("row", 0),), 2 * STEPS)
    depth_full = depth_ext.astype(jnp.float32) / 100.0
    current = fields
    for _ in range(CYCLES):
        padded = extended(current, (("row", 2),), 2 * STEPS)
        for step_no in range(STEPS):
            width = 2 * (STEPS - step_no)
            first_rate = rates(padded, trim_depth(depth_full, width))
            rows_now = padded.shape[2]
            middle = padded[:, :, 1 : rows_now - 1] + time_step * first_rate
            second_rate = rates(middle, trim_depth(depth_full, width - 1))
            rows_mid = first_rate.shape[2]
            padded = padded[:, :, 2 : rows_now - 2] + 0.5 * time_step * (
                first_rate[:, :, 1 : rows_mid - 1] + second_rate
            )
        current = padded
    sources = jnp.arange(copy_lists.shape[2], dtype=jnp.int32)
    for cycle_no in reversed(range(copy_lists.shape[0])):
        for section_no in reversed(range(copy_lists.shape[1])):
            sources = jnp.take(copy_lists[cycle_no, section_no], sources)
    spread = lax.all_to_all(current, "member", split_axis=3, concat_axis=0, tiled=True)
    return lax.all_to_all(
        jnp.take(spread, sources, axis=0), "member", split_axis=0, concat_axis=3, tiled=True
    )


def advance(state, flux, depth, target, target_flux, base, scale, col, rows, lane):
    cols = state.shape[2] // LANES
    here = pl.ds(col * LANES, LANES)
    left = pl.ds((col - 1) % cols * LANES, LANES)
    right = pl.ds((col + 1) % cols * LANES, LANES)

    def from_left(ref):
        return pltpu.roll(jnp.where(lane == LANES - 1, ref[:, left], ref[:, here]), 1, 1)

    def from_right(ref):
        return pltpu.roll(jnp.where(lane == 0, ref[:, right], ref[:, here]), LANES - 1, 1)

    height = state[0, :, here]
    east = state[1, :, here]
    north = state[2, :, here]
    rest = depth[:, here]
    flux_y = (rest + height) * north
    diff_x = from_right(flux) - from_left(flux)
    diff_y = pltpu.roll(flux_y, rows - 1, 0) - pltpu.roll(flux_y, 1, 0)
    slope_x = from_right(state.at[0]) - from_left(state.at[0])
    slope_y = pltpu.roll(height, rows - 1, 0) - pltpu.roll(height, 1, 0)
    keep = 1.0 if base is None else 0.5
    drag = keep - scale * friction
    turn = scale * coriolis
    push = 0.5 * gravity * scale
    new_h = (height if base is None else 0.5 * height) - (0.5 * scale) * (diff_x + diff_y)
    new_u = drag * east + turn * north - push * slope_x
    new_v = drag * north - turn * east - push * slope_y
    if base is not None:
        new_h = new_h + 0.5 * base[0, :, here]
        new_u = new_u + 0.5 * base[1, :, here]
        new_v = new_v + 0.5 * base[2, :, here]
    target[0, :, here] = new_h
    target[1, :, here] = new_u
    target[2, :, here] = new_v
    target_flux[:, here] = (rest + new_h) * new_u


def kernel(
    members_axis, rows_axis, fields, bathymetry, lists, out,
    state, middle, flux, flux_mid, resting, depth, held, picked, sources,
    load_sem, swap_send, swap_recv, spread_send, spread_recv, back_send, back_recv,
):
    group, row_no = lax.axis_index("member"), lax.axis_index("row")
    devices = members_axis * rows_axis
    me = group * rows_axis + row_no
    tile_rows, width = fields.shape[2], fields.shape[3]
    rows = tile_rows * rows_axis
    cols = width // LANES
    local = fields.shape[0]
    part = held.shape[2]
    own_rows = pl.ds(pl.multiple_of(row_no * tile_rows, SUBLANES), tile_rows)

    own_fields = pltpu.make_async_copy(fields.at[row_no], state.at[:, own_rows], load_sem.at[0])
    own_depth = pltpu.make_async_copy(bathymetry, resting.at[own_rows], load_sem.at[1])
    own_fields.start()
    own_depth.start()

    barrier = pltpu.get_barrier_semaphore()

    def greet(k, carry):
        other = lax.rem(me + k, devices)
        pl.semaphore_signal(
            barrier, inc=1, device_id=(other // rows_axis, lax.rem(other, rows_axis)),
            device_id_type=MESH,
        )
        return carry

    lax.fori_loop(1, devices, greet, 0)
    pl.semaphore_wait(barrier, devices - 1)

    swaps = []
    for k in range(1, rows_axis):
        other = lax.rem(row_no + k, rows_axis)
        for n, (src, dst) in enumerate(
            ((bathymetry, resting.at[own_rows]), (fields.at[other], state.at[:, own_rows]))
        ):
            copy = pltpu.make_async_remote_copy(
                src_ref=src, dst_ref=dst,
                send_sem=swap_send.at[2 * k + n], recv_sem=swap_recv.at[2 * k + n],
                device_id=(group, other), device_id_type=MESH,
            )
            copy.start()
            swaps.append(copy)
    own_fields.wait()
    own_depth.wait()
    for copy in swaps:
        copy.wait()

    depth[...] = resting[...].astype(jnp.float32) / 100.0
    flux[...] = (depth[...] + state[0]) * state[1]
    lane = lax.broadcasted_iota(jnp.int32, (rows, LANES), 1)

    def step(_, carry):
        for col in range(cols):
            advance(state, flux, depth, middle, flux_mid, None, time_step, col, rows, lane)
        for col in range(cols):
            advance(middle, flux_mid, depth, state, flux, state, 0.5 * time_step, col, rows, lane)
        return carry

    lax.fori_loop(0, STEPS * CYCLES, step, 0)

    def piece(j, r):
        return state.at[
            :,
            pl.ds(pl.multiple_of(r * tile_rows + j // cols * part, SUBLANES), part),
            pl.ds(pl.multiple_of(lax.rem(j, cols) * LANES, LANES), LANES),
        ]

    def spread_copy(other):
        j, r = other // rows_axis, lax.rem(other, rows_axis)
        return pltpu.make_async_remote_copy(
            src_ref=piece(j, r), dst_ref=held.at[me],
            send_sem=spread_send.at[other], recv_sem=spread_recv,
            device_id=(j, r), device_id_type=MESH,
        )

    half = devices // 2
    side, seat = me // half, lax.rem(me, half)

    def start_far(k, carry):
        spread_copy((1 - side) * half + lax.rem(seat + k, half)).start()
        return carry

    def start_near(k, carry):
        spread_copy(side * half + lax.rem(seat + k, half)).start()
        return carry

    lax.fori_loop(0, half, start_far, 0)
    lax.fori_loop(1, half, start_near, 0)
    pltpu.make_async_copy(piece(group, row_no), held.at[me], spread_recv).start()

    def compose(m, carry):
        source = m
        for cycle_no in reversed(range(lists.shape[1])):
            for section_no in reversed(range(lists.shape[0])):
                source = lists[section_no, cycle_no, source]
        sources[m] = source
        return carry

    lax.fori_loop(0, held.shape[0], compose, 0)
    pltpu.make_async_copy(held, held, spread_recv).wait()

    for m in range(held.shape[0]):
        picked[m] = held[sources[m]]

    place = out.at[
        :,
        :,
        pl.ds(pl.multiple_of(group // cols * part, SUBLANES), part),
        pl.ds(pl.multiple_of(lax.rem(group, cols) * LANES, LANES), LANES),
    ]

    def back_copy(k):
        other = lax.rem(group + k, members_axis)
        return pltpu.make_async_remote_copy(
            src_ref=picked.at[pl.ds(other * local, local)], dst_ref=place,
            send_sem=back_send.at[k], recv_sem=back_recv,
            device_id=(other, row_no), device_id_type=MESH,
        )

    back_half = members_axis // 2

    def start_back(k, carry):
        back_copy(lax.rem(back_half + k, members_axis)).start()
        return carry

    lax.fori_loop(0, back_half, start_back, 0)
    lax.fori_loop(back_half + 1, members_axis, start_back, 0)
    pltpu.make_async_copy(picked.at[pl.ds(group * local, local)], place, back_recv).start()

    def end_spread(k, carry):
        spread_copy(lax.rem(me + k, devices)).wait_send()
        return carry

    lax.fori_loop(1, devices, end_spread, 0)

    def end_back(k, carry):
        back_copy(k).wait_send()
        return carry

    lax.fori_loop(1, members_axis, end_back, 0)
    pltpu.make_async_copy(out, out, back_recv).wait()


def fast_body(members_axis, rows_axis, fields, bathymetry, copy_lists):
    local, kinds, tile_rows, width = fields.shape
    rows = tile_rows * rows_axis
    part = tile_rows // (members_axis // (width // LANES))
    f32 = jnp.float32
    dma = pltpu.SemaphoreType.DMA
    return pl.pallas_call(
        functools.partial(kernel, members_axis, rows_axis),
        out_shape=jax.ShapeDtypeStruct(fields.shape, f32),
        in_specs=[
            pl.BlockSpec(memory_space=pltpu.HBM),
            pl.BlockSpec(memory_space=pltpu.HBM),
            pl.BlockSpec(memory_space=pltpu.SMEM),
        ],
        out_specs=pl.BlockSpec(memory_space=pltpu.VMEM),
        scratch_shapes=[
            pltpu.VMEM((kinds, rows, width), f32),
            pltpu.VMEM((kinds, rows, width), f32),
            pltpu.VMEM((rows, width), f32),
            pltpu.VMEM((rows, width), f32),
            pltpu.VMEM((rows, width), jnp.int32),
            pltpu.VMEM((rows, width), f32),
            pltpu.VMEM((members_axis * local, kinds, part, LANES), f32),
            pltpu.VMEM((members_axis * local, kinds, part, LANES), f32),
            pltpu.SMEM((members_axis * local,), jnp.int32),
            dma((2,)),
            dma((2 * rows_axis,)),
            dma((2 * rows_axis,)),
            dma((members_axis * rows_axis,)),
            dma,
            dma((members_axis,)),
            dma,
        ],
        compiler_params=pltpu.CompilerParams(
            collective_id=0, has_side_effects=True, vmem_limit_bytes=32 * 1024 * 1024
        ),
    )(fields, bathymetry, jnp.swapaxes(copy_lists, 0, 1))


def solution(mesh):
    members_axis, rows_axis = mesh.shape["member"], mesh.shape["row"]
    placed = (P("member", None, "row", None), P("row", None), P())

    def body(fields, bathymetry, copy_lists):
        local, _, tile_rows, width = fields.shape
        cols = width // LANES
        splits = max(members_axis // cols, 1)
        fits = (
            local == rows_axis
            and width % LANES == 0
            and members_axis % cols == 0
            and members_axis % 2 == 0
            and tile_rows % (splits * SUBLANES) == 0
        )
        if fits:
            return fast_body(members_axis, rows_axis, fields, bathymetry, copy_lists)
        return general_body(fields, bathymetry, copy_lists)

    return jax.shard_map(
        body, mesh=mesh, in_specs=placed, out_specs=P("member", None, "row", None), check_vma=False
    )
```

```python
import functools

import jax
import jax.numpy as jnp
from jax import lax
from jax.experimental import pallas as pl
from jax.experimental.pallas import tpu as pltpu
from jax.sharding import PartitionSpec as P

STEPS = 4
CYCLES = 3


gravity = 2.0
coriolis = 0.1
friction = 0.02
time_step = 0.25

LANES = 128
SUBLANES = 8
MESH = pl.DeviceIdType.MESH


def extended(x, sides, width):
    for axis, dim in sides:
        devices, length = (lax.axis_size(axis), x.shape[dim])
        up = [(i, (i + 1) % devices) for i in range(devices)]
        down = [(j, i) for i, j in up]
        last = lax.slice_in_dim(x, length - width, length, axis=dim)
        leading = lax.slice_in_dim(x, 0, width, axis=dim)
        before = lax.ppermute(last, axis, up)
        after = lax.ppermute(leading, axis, down)
        x = jnp.concatenate([before, x, after], axis=dim)
    return x


def rates(padded, depth_pad):
    height = padded[:, 0]
    east = padded[:, 1]
    north = padded[:, 2]
    column = depth_pad + height
    flux_x = column * east
    flux_y = column * north
    diff_x = (jnp.roll(flux_x, -1, -1) - jnp.roll(flux_x, 1, -1))[:, 1:-1]
    diff_y = flux_y[:, 2:] - flux_y[:, :-2]
    rate_h = -0.5 * (diff_x + diff_y)
    slope_x = (jnp.roll(height, -1, -1) - jnp.roll(height, 1, -1))[:, 1:-1]
    slope_y = height[:, 2:] - height[:, :-2]
    east_mid = east[:, 1:-1]
    north_mid = north[:, 1:-1]
    rate_u = -0.5 * gravity * slope_x + coriolis * north_mid - friction * east_mid
    rate_v = -0.5 * gravity * slope_y - coriolis * east_mid - friction * north_mid
    return jnp.stack([rate_h, rate_u, rate_v], 1)


def trim_depth(depth_full, width):
    offset = 2 * STEPS - width
    total = depth_full.shape[0]
    return depth_full[offset : total - offset]


def general_body(fields, bathymetry, copy_lists):
    depth_ext = extended(bathymetry, (("row", 0),), 2 * STEPS)
    depth_full = depth_ext.astype(jnp.float32) / 100.0
    current = fields
    for _ in range(CYCLES):
        padded = extended(current, (("row", 2),), 2 * STEPS)
        for step_no in range(STEPS):
            width = 2 * (STEPS - step_no)
            first_rate = rates(padded, trim_depth(depth_full, width))
            rows_now = padded.shape[2]
            middle = padded[:, :, 1 : rows_now - 1] + time_step * first_rate
            second_rate = rates(middle, trim_depth(depth_full, width - 1))
            rows_mid = first_rate.shape[2]
            padded = padded[:, :, 2 : rows_now - 2] + 0.5 * time_step * (
                first_rate[:, :, 1 : rows_mid - 1] + second_rate
            )
        current = padded
    sources = jnp.arange(copy_lists.shape[2], dtype=jnp.int32)
    for cycle_no in reversed(range(copy_lists.shape[0])):
        for section_no in reversed(range(copy_lists.shape[1])):
            sources = jnp.take(copy_lists[cycle_no, section_no], sources)
    spread = lax.all_to_all(current, "member", split_axis=3, concat_axis=0, tiled=True)
    return lax.all_to_all(
        jnp.take(spread, sources, axis=0), "member", split_axis=0, concat_axis=3, tiled=True
    )


def advance(state, flux, depth, target, target_flux, base, scale, col, rows, lane):
    cols = state.shape[2] // LANES
    here = pl.ds(col * LANES, LANES)
    left = pl.ds((col - 1) % cols * LANES, LANES)
    right = pl.ds((col + 1) % cols * LANES, LANES)

    def from_left(ref):
        return pltpu.roll(jnp.where(lane == LANES - 1, ref[:, left], ref[:, here]), 1, 1)

    def from_right(ref):
        return pltpu.roll(jnp.where(lane == 0, ref[:, right], ref[:, here]), LANES - 1, 1)

    height = state[0, :, here]
    east = state[1, :, here]
    north = state[2, :, here]
    rest = depth[:, here]
    flux_y = (rest + height) * north
    diff_x = from_right(flux) - from_left(flux)
    diff_y = pltpu.roll(flux_y, rows - 1, 0) - pltpu.roll(flux_y, 1, 0)
    slope_x = from_right(state.at[0]) - from_left(state.at[0])
    slope_y = pltpu.roll(height, rows - 1, 0) - pltpu.roll(height, 1, 0)
    keep = 1.0 if base is None else 0.5
    drag = keep - scale * friction
    turn = scale * coriolis
    push = 0.5 * gravity * scale
    new_h = (height if base is None else 0.5 * height) - (0.5 * scale) * (diff_x + diff_y)
    new_u = drag * east + turn * north - push * slope_x
    new_v = drag * north - turn * east - push * slope_y
    if base is not None:
        new_h = new_h + 0.5 * base[0, :, here]
        new_u = new_u + 0.5 * base[1, :, here]
        new_v = new_v + 0.5 * base[2, :, here]
    target[0, :, here] = new_h
    target[1, :, here] = new_u
    target[2, :, here] = new_v
    target_flux[:, here] = (rest + new_h) * new_u


def kernel(
    members_axis, rows_axis, fields, bathymetry, lists_in, out,
    state, middle, flux, flux_mid, resting, depth, held, picked, lists, sources,
    load_sem, swap_send, swap_recv, spread_send, spread_recv, back_send, back_recv,
):
    group, row_no = lax.axis_index("member"), lax.axis_index("row")
    devices = members_axis * rows_axis
    me = group * rows_axis + row_no
    tile_rows, width = fields.shape[2], fields.shape[3]
    rows = tile_rows * rows_axis
    cols = width // LANES
    local = fields.shape[0]
    part = held[0].shape[1]
    own_rows = pl.ds(pl.multiple_of(row_no * tile_rows, SUBLANES), tile_rows)

    own_fields = pltpu.make_async_copy(fields.at[row_no], state.at[:, own_rows], load_sem.at[0])
    own_depth = pltpu.make_async_copy(bathymetry, resting.at[own_rows], load_sem.at[1])
    own_lists = pltpu.make_async_copy(lists_in, lists, load_sem.at[2])
    own_fields.start()
    own_depth.start()
    own_lists.start()

    barrier = pltpu.get_barrier_semaphore()

    def greet(k, carry):
        other = lax.rem(me + k, devices)
        pl.semaphore_signal(
            barrier, inc=1, device_id=(other // rows_axis, lax.rem(other, rows_axis)),
            device_id_type=MESH,
        )
        return carry

    lax.fori_loop(1, devices, greet, 0)
    pl.semaphore_wait(barrier, devices - 1)

    swaps = []
    for k in range(1, rows_axis):
        other = lax.rem(row_no + k, rows_axis)
        for n, (src, dst) in enumerate(
            ((bathymetry, resting.at[own_rows]), (fields.at[other], state.at[:, own_rows]))
        ):
            copy = pltpu.make_async_remote_copy(
                src_ref=src, dst_ref=dst,
                send_sem=swap_send.at[2 * k + n], recv_sem=swap_recv.at[2 * k + n],
                device_id=(group, other), device_id_type=MESH,
            )
            copy.start()
            swaps.append(copy)
    own_fields.wait()
    own_depth.wait()
    for copy in swaps:
        copy.wait()

    depth[...] = resting[...].astype(jnp.float32) / 100.0
    flux[...] = (depth[...] + state[0]) * state[1]
    lane = lax.broadcasted_iota(jnp.int32, (rows, LANES), 1)

    def step(_, carry):
        for col in range(cols):
            advance(state, flux, depth, middle, flux_mid, None, time_step, col, rows, lane)
        for col in range(cols):
            advance(middle, flux_mid, depth, state, flux, state, 0.5 * time_step, col, rows, lane)
        return carry

    lax.fori_loop(0, STEPS * CYCLES, step, 0)

    def piece(kind, j, r):
        return state.at[
            kind,
            pl.ds(pl.multiple_of(r * tile_rows + j // cols * part, SUBLANES), part),
            pl.ds(pl.multiple_of(lax.rem(j, cols) * LANES, LANES), LANES),
        ]

    def spread_copy(kind, other):
        j, r = other // rows_axis, lax.rem(other, rows_axis)
        return pltpu.make_async_remote_copy(
            src_ref=piece(kind, j, r), dst_ref=held[kind].at[me],
            send_sem=spread_send.at[kind, other], recv_sem=spread_recv.at[kind],
            device_id=(j, r), device_id_type=MESH,
        )

    half = devices // 2
    side, seat = me // half, lax.rem(me, half)
    far, near = (1 - side) * half, side * half
    kinds = state.shape[0]

    for kind in range(kinds):
        spread_copy(kind, far + seat).start()

        def start_spread(k, carry, kind=kind):
            there = lax.rem(seat + k, half)
            spread_copy(kind, far + there).start()
            spread_copy(kind, near + there).start()
            return carry

        lax.fori_loop(1, half, start_spread, 0)
        pltpu.make_async_copy(
            piece(kind, group, row_no), held[kind].at[me], spread_recv.at[kind]
        ).start()

    own_lists.wait()

    def compose(m, carry):
        source = m
        for cycle_no in reversed(range(lists.shape[1])):
            for section_no in reversed(range(lists.shape[0])):
                source = lists[section_no, cycle_no, source]
        sources[m] = source
        return carry

    lax.fori_loop(0, sources.shape[0], compose, 0)

    def place(kind):
        return out.at[
            :,
            kind,
            pl.ds(pl.multiple_of(group // cols * part, SUBLANES), part),
            pl.ds(pl.multiple_of(lax.rem(group, cols) * LANES, LANES), LANES),
        ]

    def back_copy(kind, other):
        return pltpu.make_async_remote_copy(
            src_ref=picked[kind].at[pl.ds(other * local, local)], dst_ref=place(kind),
            send_sem=back_send.at[kind, other], recv_sem=back_recv.at[kind],
            device_id=(other, row_no), device_id_type=MESH,
        )

    back_half = members_axis // 2
    back_side, back_seat = group // back_half, lax.rem(group, back_half)
    back_far, back_near = (1 - back_side) * back_half, back_side * back_half

    for kind in range(kinds):
        pltpu.make_async_copy(held[kind], held[kind], spread_recv.at[kind]).wait()
        for m in range(sources.shape[0]):
            picked[kind][m] = held[kind][sources[m]]
        back_copy(kind, back_far + back_seat).start()

        def start_back(k, carry, kind=kind):
            there = lax.rem(back_seat + k, back_half)
            back_copy(kind, back_far + there).start()
            back_copy(kind, back_near + there).start()
            return carry

        lax.fori_loop(1, back_half, start_back, 0)
        pltpu.make_async_copy(
            picked[kind].at[pl.ds(group * local, local)], place(kind), back_recv.at[kind]
        ).start()

    for kind in range(kinds):

        def end_spread(k, carry, kind=kind):
            spread_copy(kind, lax.rem(me + k, devices)).wait_send()
            return carry

        lax.fori_loop(1, devices, end_spread, 0)

        def end_back(k, carry, kind=kind):
            back_copy(kind, lax.rem(group + k, members_axis)).wait_send()
            return carry

        lax.fori_loop(1, members_axis, end_back, 0)
    for kind in range(kinds):
        pltpu.make_async_copy(out.at[:, kind], out.at[:, kind], back_recv.at[kind]).wait()


def fast_body(members_axis, rows_axis, fields, bathymetry, copy_lists):
    local, kinds, tile_rows, width = fields.shape
    rows = tile_rows * rows_axis
    part = tile_rows // (members_axis // (width // LANES))
    f32 = jnp.float32
    dma = pltpu.SemaphoreType.DMA
    return pl.pallas_call(
        functools.partial(kernel, members_axis, rows_axis),
        out_shape=jax.ShapeDtypeStruct(fields.shape, f32),
        in_specs=[
            pl.BlockSpec(memory_space=pltpu.HBM),
            pl.BlockSpec(memory_space=pltpu.HBM),
            pl.BlockSpec(memory_space=pltpu.HBM),
        ],
        out_specs=pl.BlockSpec(memory_space=pltpu.VMEM),
        scratch_shapes=[
            pltpu.VMEM((kinds, rows, width), f32),
            pltpu.VMEM((kinds, rows, width), f32),
            pltpu.VMEM((rows, width), f32),
            pltpu.VMEM((rows, width), f32),
            pltpu.VMEM((rows, width), jnp.int32),
            pltpu.VMEM((rows, width), f32),
            [pltpu.VMEM((members_axis * local, part, LANES), f32)] * kinds,
            [pltpu.VMEM((members_axis * local, part, LANES), f32)] * kinds,
            pltpu.SMEM((copy_lists.shape[1], copy_lists.shape[0], copy_lists.shape[2]), jnp.int32),
            pltpu.SMEM((members_axis * local,), jnp.int32),
            dma((3,)),
            dma((2 * rows_axis,)),
            dma((2 * rows_axis,)),
            dma((kinds, members_axis * rows_axis)),
            dma((kinds,)),
            dma((kinds, members_axis)),
            dma((kinds,)),
        ],
        compiler_params=pltpu.CompilerParams(
            collective_id=0, has_side_effects=True
        ),
    )(fields, bathymetry, jnp.swapaxes(copy_lists, 0, 1))


def solution(mesh):
    members_axis, rows_axis = mesh.shape["member"], mesh.shape["row"]
    placed = (P("member", None, "row", None), P("row", None), P())

    def body(fields, bathymetry, copy_lists):
        local, _, tile_rows, width = fields.shape
        cols = width // LANES
        splits = max(members_axis // cols, 1)
        fits = (
            local == rows_axis
            and width % LANES == 0
            and members_axis % cols == 0
            and members_axis % 2 == 0
            and tile_rows % (splits * SUBLANES) == 0
        )
        if fits:
            return fast_body(members_axis, rows_axis, fields, bathymetry, copy_lists)
        return general_body(fields, bathymetry, copy_lists)

    return jax.shard_map(
        body, mesh=mesh, in_specs=placed, out_specs=P("member", None, "row", None), check_vma=False
    )
```

```python
import functools

import jax
import jax.numpy as jnp
from jax import lax
from jax.experimental import pallas as pl
from jax.experimental.pallas import tpu as pltpu
from jax.sharding import PartitionSpec as P

STEPS = 4
CYCLES = 3


gravity = 2.0
coriolis = 0.1
friction = 0.02
time_step = 0.25

LANES = 128
SUBLANES = 8
MESH = pl.DeviceIdType.MESH
LAG = 2


def extended(x, sides, width):
    for axis, dim in sides:
        devices, length = (lax.axis_size(axis), x.shape[dim])
        up = [(i, (i + 1) % devices) for i in range(devices)]
        down = [(j, i) for i, j in up]
        last = lax.slice_in_dim(x, length - width, length, axis=dim)
        leading = lax.slice_in_dim(x, 0, width, axis=dim)
        before = lax.ppermute(last, axis, up)
        after = lax.ppermute(leading, axis, down)
        x = jnp.concatenate([before, x, after], axis=dim)
    return x


def rates(padded, depth_pad):
    height = padded[:, 0]
    east = padded[:, 1]
    north = padded[:, 2]
    column = depth_pad + height
    flux_x = column * east
    flux_y = column * north
    diff_x = (jnp.roll(flux_x, -1, -1) - jnp.roll(flux_x, 1, -1))[:, 1:-1]
    diff_y = flux_y[:, 2:] - flux_y[:, :-2]
    rate_h = -0.5 * (diff_x + diff_y)
    slope_x = (jnp.roll(height, -1, -1) - jnp.roll(height, 1, -1))[:, 1:-1]
    slope_y = height[:, 2:] - height[:, :-2]
    east_mid = east[:, 1:-1]
    north_mid = north[:, 1:-1]
    rate_u = -0.5 * gravity * slope_x + coriolis * north_mid - friction * east_mid
    rate_v = -0.5 * gravity * slope_y - coriolis * east_mid - friction * north_mid
    return jnp.stack([rate_h, rate_u, rate_v], 1)


def trim_depth(depth_full, width):
    offset = 2 * STEPS - width
    total = depth_full.shape[0]
    return depth_full[offset : total - offset]


def general_body(fields, bathymetry, copy_lists):
    depth_ext = extended(bathymetry, (("row", 0),), 2 * STEPS)
    depth_full = depth_ext.astype(jnp.float32) / 100.0
    current = fields
    for _ in range(CYCLES):
        padded = extended(current, (("row", 2),), 2 * STEPS)
        for step_no in range(STEPS):
            width = 2 * (STEPS - step_no)
            first_rate = rates(padded, trim_depth(depth_full, width))
            rows_now = padded.shape[2]
            middle = padded[:, :, 1 : rows_now - 1] + time_step * first_rate
            second_rate = rates(middle, trim_depth(depth_full, width - 1))
            rows_mid = first_rate.shape[2]
            padded = padded[:, :, 2 : rows_now - 2] + 0.5 * time_step * (
                first_rate[:, :, 1 : rows_mid - 1] + second_rate
            )
        current = padded
    sources = jnp.arange(copy_lists.shape[2], dtype=jnp.int32)
    for cycle_no in reversed(range(copy_lists.shape[0])):
        for section_no in reversed(range(copy_lists.shape[1])):
            sources = jnp.take(copy_lists[cycle_no, section_no], sources)
    spread = lax.all_to_all(current, "member", split_axis=3, concat_axis=0, tiled=True)
    return lax.all_to_all(
        jnp.take(spread, sources, axis=0), "member", split_axis=0, concat_axis=3, tiled=True
    )


def advance(state, flux, depth, target, target_flux, base, scale, col, rows, lane):
    cols = state.shape[2] // LANES
    here = pl.ds(col * LANES, LANES)
    left = pl.ds((col - 1) % cols * LANES, LANES)
    right = pl.ds((col + 1) % cols * LANES, LANES)

    def from_left(ref):
        return pltpu.roll(jnp.where(lane == LANES - 1, ref[:, left], ref[:, here]), 1, 1)

    def from_right(ref):
        return pltpu.roll(jnp.where(lane == 0, ref[:, right], ref[:, here]), LANES - 1, 1)

    height = state[0, :, here]
    east = state[1, :, here]
    north = state[2, :, here]
    rest = depth[:, here]
    flux_y = (rest + height) * north
    diff_x = from_right(flux) - from_left(flux)
    diff_y = pltpu.roll(flux_y, rows - 1, 0) - pltpu.roll(flux_y, 1, 0)
    slope_x = from_right(state.at[0]) - from_left(state.at[0])
    slope_y = pltpu.roll(height, rows - 1, 0) - pltpu.roll(height, 1, 0)
    keep = 1.0 if base is None else 0.5
    drag = keep - scale * friction
    turn = scale * coriolis
    push = 0.5 * gravity * scale
    new_h = (height if base is None else 0.5 * height) - (0.5 * scale) * (diff_x + diff_y)
    new_u = drag * east + turn * north - push * slope_x
    new_v = drag * north - turn * east - push * slope_y
    if base is not None:
        new_h = new_h + 0.5 * base[0, :, here]
        new_u = new_u + 0.5 * base[1, :, here]
        new_v = new_v + 0.5 * base[2, :, here]
    target[0, :, here] = new_h
    target[1, :, here] = new_u
    target[2, :, here] = new_v
    target_flux[:, here] = (rest + new_h) * new_u


def alternate(count):
    half = count // 2
    return [k for pair in zip(range(half, count), [*range(1, half), 0]) for k in pair]


def kernel(
    members_axis, rows_axis, fields, bathymetry, lists_in, out,
    state, resting, work, middle, flux, flux_mid, depth, held, picked, lists, sources,
    load_sem, swap_send, swap_recv, spread_send, spread_recv, back_send, back_recv,
):
    group, row_no = lax.axis_index("member"), lax.axis_index("row")
    devices = members_axis * rows_axis
    me = group * rows_axis + row_no
    local, kinds, tile_rows, width = fields.shape
    rows = tile_rows * rows_axis
    cols = width // LANES
    chunks = work.shape[0]
    chunk_cols = cols // chunks
    per_chunk = members_axis // 2
    members = members_axis * local
    own_rows = pl.ds(pl.multiple_of(row_no * tile_rows, SUBLANES), tile_rows)

    own_fields = pltpu.make_async_copy(fields.at[row_no], state.at[:, own_rows], load_sem.at[0])
    own_depth = pltpu.make_async_copy(bathymetry, resting.at[own_rows], load_sem.at[1])
    own_lists = pltpu.make_async_copy(lists_in, lists, load_sem.at[2])
    own_fields.start()
    own_depth.start()
    own_lists.start()

    barrier = pltpu.get_barrier_semaphore()

    def greet(k, carry):
        other = lax.rem(me + k, devices)
        pl.semaphore_signal(
            barrier, inc=1, device_id=(other // rows_axis, lax.rem(other, rows_axis)),
            device_id_type=MESH,
        )
        return carry

    lax.fori_loop(1, devices, greet, 0)
    pl.semaphore_wait(barrier, devices - 1)

    swaps = []
    for k in range(1, rows_axis):
        other = lax.rem(row_no + k, rows_axis)
        for n, (src, dst) in enumerate(
            ((bathymetry, resting.at[own_rows]), (fields.at[other], state.at[:, own_rows]))
        ):
            copy = pltpu.make_async_remote_copy(
                src_ref=src, dst_ref=dst,
                send_sem=swap_send.at[2 * k + n], recv_sem=swap_recv.at[2 * k + n],
                device_id=(group, other), device_id_type=MESH,
            )
            copy.start()
            swaps.append(copy)
    own_fields.wait()
    own_depth.wait()
    own_lists.wait()
    for copy in swaps:
        copy.wait()

    lane = lax.broadcasted_iota(jnp.int32, (rows, LANES), 1)
    steps = STEPS * CYCLES
    share = -(-members // steps)

    def compose(m):
        source = m
        for cycle_no in reversed(range(lists.shape[1])):
            for section_no in reversed(range(lists.shape[0])):
                source = lists[section_no, cycle_no, source]
        sources[m] = source

    def forecast(q):
        first = q * chunk_cols
        chunk = work.at[q]
        for col in range(chunk_cols + 1):
            here = pl.ds(col * LANES, LANES)
            if col < chunk_cols:
                source = pl.ds((first + col) * LANES, LANES)
                tile = [state[kind, :, source] for kind in range(kinds)]
                rest = resting[:, source]
            else:
                after = pl.ds((first + col) % cols * LANES, LANES)
                before = pl.ds((first - 1) % cols * LANES, LANES)
                follows = lane < LANES // 2
                tile = [
                    jnp.where(follows, state[kind, :, after], state[kind, :, before])
                    for kind in range(kinds)
                ]
                rest = jnp.where(follows, resting[:, after], resting[:, before])
            rest = rest.astype(jnp.float32) / 100.0
            depth[:, here] = rest
            for kind in range(kinds):
                chunk[kind, :, here] = tile[kind]
            flux[:, here] = (rest + tile[0]) * tile[1]

        def step(i, carry):
            if q == 0:
                for n in range(share):
                    compose(jnp.minimum(i * share + n, members - 1))
            for col in range(chunk_cols + 1):
                advance(chunk, flux, depth, middle, flux_mid, None, time_step, col, rows, lane)
            for col in range(chunk_cols + 1):
                advance(
                    middle, flux_mid, depth, chunk, flux, chunk, 0.5 * time_step, col, rows, lane
                )
            return carry

        lax.fori_loop(0, steps, step, 0)

    seat = group // 2

    def spread_copy(q, n, offset):
        t = lax.rem(seat + offset, per_chunk)
        j, r = 2 * t + lax.rem(t + q, 2), q // 2
        src = work.at[
            q,
            :,
            pl.ds(pl.multiple_of(t // chunk_cols * SUBLANES, SUBLANES), SUBLANES),
            pl.ds(pl.multiple_of(lax.rem(t, chunk_cols) * LANES, LANES), LANES),
        ]
        remote = pltpu.make_async_remote_copy(
            src_ref=src, dst_ref=held.at[me],
            send_sem=spread_send.at[q, n], recv_sem=spread_recv,
            device_id=(j, r), device_id_type=MESH,
        )
        return remote, src, j * rows_axis + r

    def spread(q):
        for n, offset in enumerate(alternate(per_chunk)):
            remote, src, target = spread_copy(q, n, offset)
            if offset:
                remote.start()
                continue

            @pl.when(target != me)
            def _():
                remote.start()

            @pl.when(target == me)
            def _():
                pltpu.make_async_copy(src, held.at[me], spread_recv).start()

    my_chunk = 2 * row_no + lax.rem(group + seat, 2)
    my_row = seat // chunk_cols * SUBLANES
    home = my_row // tile_rows
    place = out.at[
        :,
        :,
        pl.ds(pl.multiple_of(lax.rem(my_row, tile_rows), SUBLANES), SUBLANES),
        pl.ds(
            pl.multiple_of((my_chunk * chunk_cols + lax.rem(seat, chunk_cols)) * LANES, LANES),
            LANES,
        ),
    ]

    def back_copy(n, offset):
        other = lax.rem(group + offset, members_axis)
        src = picked.at[pl.ds(other * local, local)]
        return src, pltpu.make_async_remote_copy(
            src_ref=src, dst_ref=place,
            send_sem=back_send.at[n], recv_sem=back_recv,
            device_id=(other, home), device_id_type=MESH,
        )

    def give_back():
        pltpu.make_async_copy(held, held, spread_recv).wait()
        for m in range(members):
            picked[m] = held[sources[m]]
        for n, offset in enumerate(alternate(members_axis)):
            src, remote = back_copy(n, offset)
            if offset:
                remote.start()
                continue

            @pl.when(home != row_no)
            def _():
                remote.start()

            @pl.when(home == row_no)
            def _():
                pltpu.make_async_copy(src, place, back_recv).start()

    for q in range(chunks + LAG):
        if q < chunks:
            forecast(q)
            spread(q)
        if q >= LAG:

            @pl.when(my_chunk == q - LAG)
            def _():
                give_back()

    for q in range(chunks):
        for n, offset in enumerate(alternate(per_chunk)):
            remote, _, target = spread_copy(q, n, offset)
            if offset:
                remote.wait_send()
                continue

            @pl.when(target != me)
            def _():
                remote.wait_send()

    for n, offset in enumerate(alternate(members_axis)):
        _, remote = back_copy(n, offset)
        if offset:
            remote.wait_send()
            continue

        @pl.when(home != row_no)
        def _():
            remote.wait_send()

    pltpu.make_async_copy(out, out, back_recv).wait()


def fast_body(members_axis, rows_axis, fields, bathymetry, copy_lists):
    local, kinds, tile_rows, width = fields.shape
    rows = tile_rows * rows_axis
    chunks = 2 * rows_axis
    chunk_width = width // chunks + LANES
    members = members_axis * local
    f32 = jnp.float32
    dma = pltpu.SemaphoreType.DMA
    return pl.pallas_call(
        functools.partial(kernel, members_axis, rows_axis),
        out_shape=jax.ShapeDtypeStruct(fields.shape, f32),
        in_specs=[pl.BlockSpec(memory_space=pltpu.HBM)] * 3,
        out_specs=pl.BlockSpec(memory_space=pltpu.HBM),
        scratch_shapes=[
            pltpu.VMEM((kinds, rows, width), f32),
            pltpu.VMEM((rows, width), jnp.int32),
            pltpu.VMEM((chunks, kinds, rows, chunk_width), f32),
            pltpu.VMEM((kinds, rows, chunk_width), f32),
            pltpu.VMEM((rows, chunk_width), f32),
            pltpu.VMEM((rows, chunk_width), f32),
            pltpu.VMEM((rows, chunk_width), f32),
            pltpu.VMEM((members, kinds, SUBLANES, LANES), f32),
            pltpu.VMEM((members, kinds, SUBLANES, LANES), f32),
            pltpu.SMEM((copy_lists.shape[1], copy_lists.shape[0], copy_lists.shape[2]), jnp.int32),
            pltpu.SMEM((members,), jnp.int32),
            dma((3,)),
            dma((2 * rows_axis,)),
            dma((2 * rows_axis,)),
            dma((chunks, members_axis // 2)),
            dma,
            dma((members_axis,)),
            dma,
        ],
        compiler_params=pltpu.CompilerParams(collective_id=0, has_side_effects=True),
    )(fields, bathymetry, jnp.swapaxes(copy_lists, 0, 1))


def solution(mesh):
    members_axis, rows_axis = mesh.shape["member"], mesh.shape["row"]
    placed = (P("member", None, "row", None), P("row", None), P())

    def body(fields, bathymetry, copy_lists):
        local, _, tile_rows, width = fields.shape
        chunks = 2 * rows_axis
        chunk_cols = width // (LANES * chunks)
        row_tiles = tile_rows * rows_axis // SUBLANES
        fits = (
            local == rows_axis
            and width % (LANES * chunks) == 0
            and tile_rows % SUBLANES == 0
            and members_axis == 2 * row_tiles * chunk_cols
            and 2 * STEPS * CYCLES <= LANES // 2
        )
        if fits:
            return fast_body(members_axis, rows_axis, fields, bathymetry, copy_lists)
        return general_body(fields, bathymetry, copy_lists)

    return jax.shard_map(
        body, mesh=mesh, in_specs=placed, out_specs=P("member", None, "row", None), check_vma=False
    )
```

```python
import functools

import jax
import jax.numpy as jnp
from jax import lax
from jax.experimental import pallas as pl
from jax.experimental.pallas import tpu as pltpu
from jax.sharding import PartitionSpec as P

STEPS = 4
CYCLES = 3


gravity = 2.0
coriolis = 0.1
friction = 0.02
time_step = 0.25

LANES = 128
SUBLANES = 8
MESH = pl.DeviceIdType.MESH


def extended(x, sides, width):
    for axis, dim in sides:
        devices, length = (lax.axis_size(axis), x.shape[dim])
        up = [(i, (i + 1) % devices) for i in range(devices)]
        down = [(j, i) for i, j in up]
        last = lax.slice_in_dim(x, length - width, length, axis=dim)
        leading = lax.slice_in_dim(x, 0, width, axis=dim)
        before = lax.ppermute(last, axis, up)
        after = lax.ppermute(leading, axis, down)
        x = jnp.concatenate([before, x, after], axis=dim)
    return x


def rates(padded, depth_pad):
    height = padded[:, 0]
    east = padded[:, 1]
    north = padded[:, 2]
    column = depth_pad + height
    flux_x = column * east
    flux_y = column * north
    diff_x = (jnp.roll(flux_x, -1, -1) - jnp.roll(flux_x, 1, -1))[:, 1:-1]
    diff_y = flux_y[:, 2:] - flux_y[:, :-2]
    rate_h = -0.5 * (diff_x + diff_y)
    slope_x = (jnp.roll(height, -1, -1) - jnp.roll(height, 1, -1))[:, 1:-1]
    slope_y = height[:, 2:] - height[:, :-2]
    east_mid = east[:, 1:-1]
    north_mid = north[:, 1:-1]
    rate_u = -0.5 * gravity * slope_x + coriolis * north_mid - friction * east_mid
    rate_v = -0.5 * gravity * slope_y - coriolis * east_mid - friction * north_mid
    return jnp.stack([rate_h, rate_u, rate_v], 1)


def trim_depth(depth_full, width):
    offset = 2 * STEPS - width
    total = depth_full.shape[0]
    return depth_full[offset : total - offset]


def general_body(fields, bathymetry, copy_lists):
    depth_ext = extended(bathymetry, (("row", 0),), 2 * STEPS)
    depth_full = depth_ext.astype(jnp.float32) / 100.0
    current = fields
    for _ in range(CYCLES):
        padded = extended(current, (("row", 2),), 2 * STEPS)
        for step_no in range(STEPS):
            width = 2 * (STEPS - step_no)
            first_rate = rates(padded, trim_depth(depth_full, width))
            rows_now = padded.shape[2]
            middle = padded[:, :, 1 : rows_now - 1] + time_step * first_rate
            second_rate = rates(middle, trim_depth(depth_full, width - 1))
            rows_mid = first_rate.shape[2]
            padded = padded[:, :, 2 : rows_now - 2] + 0.5 * time_step * (
                first_rate[:, :, 1 : rows_mid - 1] + second_rate
            )
        current = padded
    sources = jnp.arange(copy_lists.shape[2], dtype=jnp.int32)
    for cycle_no in reversed(range(copy_lists.shape[0])):
        for section_no in reversed(range(copy_lists.shape[1])):
            sources = jnp.take(copy_lists[cycle_no, section_no], sources)
    spread = lax.all_to_all(current, "member", split_axis=3, concat_axis=0, tiled=True)
    return lax.all_to_all(
        jnp.take(spread, sources, axis=0), "member", split_axis=0, concat_axis=3, tiled=True
    )


def advance(state, flux, depth, target, target_flux, base, scale, col, lane):
    cols = state.shape[-1] // LANES
    count = state.shape[1]
    here = pl.ds(col * LANES, LANES)
    left = pl.ds((col - 1) % cols * LANES, LANES)
    right = pl.ds((col + 1) % cols * LANES, LANES)
    first_lane, last_lane = lane == 0, lane == LANES - 1

    def slope_east(ref, k):
        own = ref[k, :, here]
        after = pltpu.roll(jnp.where(first_lane, ref[k, :, right], own), LANES - 1, 1)
        before = pltpu.roll(jnp.where(last_lane, ref[k, :, left], own), 1, 1)
        return after - before

    def slope_north(tiles, k):
        after = tiles[k + 1] if k + 1 < count else pltpu.roll(tiles[0], SUBLANES - 1, 0)
        before = tiles[k - 1] if k > 0 else pltpu.roll(tiles[count - 1], 1, 0)
        return after - before

    keep = 1.0 if base is None else 0.5
    drag = keep - scale * friction
    turn = scale * coriolis
    push = 0.5 * gravity * scale
    heights = [state[0, k, :, here] for k in range(count)]
    norths = [state[2, k, :, here] for k in range(count)]
    rests = [depth[k, :, here] for k in range(count)]
    fluxes = [(rests[k] + heights[k]) * norths[k] for k in range(count)]
    for k in range(count):
        height, north, east = heights[k], norths[k], state[1, k, :, here]
        spread_out = slope_east(flux, k) + slope_north(fluxes, k)
        new_h = (height if base is None else 0.5 * height) - (0.5 * scale) * spread_out
        new_u = drag * east + turn * north - push * slope_east(state.at[0], k)
        new_v = drag * north - turn * east - push * slope_north(heights, k)
        if base is not None:
            new_h = new_h + 0.5 * base[0, k, :, here]
            new_u = new_u + 0.5 * base[1, k, :, here]
            new_v = new_v + 0.5 * base[2, k, :, here]
        target[0, k, :, here] = new_h
        target[1, k, :, here] = new_u
        target[2, k, :, here] = new_v
        target_flux[k, :, here] = (rests[k] + new_h) * new_u


def kernel(
    members_axis, rows_axis, fields, bathymetry, lists_in, out,
    state, stage, dealt, middle, flux, flux_mid, resting, depth, held, picked, lists, sources,
    load_sem, swap_send, swap_recv, spread_send, spread_recv, back_send, back_recv,
):
    group, row_no = lax.axis_index("member"), lax.axis_index("row")
    devices = members_axis * rows_axis
    me = group * rows_axis + row_no
    tile_rows, width = fields.shape[2], fields.shape[3]
    rows = tile_rows * rows_axis
    cols = width // LANES
    local = fields.shape[0]
    part = held[0].shape[1]
    own_rows = pl.ds(pl.multiple_of(row_no * tile_rows, SUBLANES), tile_rows)

    own_fields = pltpu.make_async_copy(fields.at[row_no], state.at[:, own_rows], load_sem.at[0])
    own_depth = pltpu.make_async_copy(bathymetry, resting.at[own_rows], load_sem.at[1])
    own_lists = pltpu.make_async_copy(lists_in, lists, load_sem.at[2])
    own_fields.start()
    own_depth.start()
    own_lists.start()

    barrier = pltpu.get_barrier_semaphore()

    def greet(k, carry):
        other = lax.rem(me + k, devices)
        pl.semaphore_signal(
            barrier, inc=1, device_id=(other // rows_axis, lax.rem(other, rows_axis)),
            device_id_type=MESH,
        )
        return carry

    lax.fori_loop(1, devices, greet, 0)
    pl.semaphore_wait(barrier, devices - 1)

    swaps = []
    for k in range(1, rows_axis):
        other = lax.rem(row_no + k, rows_axis)
        for n, (src, dst) in enumerate(
            ((bathymetry, resting.at[own_rows]), (fields.at[other], state.at[:, own_rows]))
        ):
            copy = pltpu.make_async_remote_copy(
                src_ref=src, dst_ref=dst,
                send_sem=swap_send.at[2 * k + n], recv_sem=swap_recv.at[2 * k + n],
                device_id=(group, other), device_id_type=MESH,
            )
            copy.start()
            swaps.append(copy)
    own_fields.wait()
    own_depth.wait()
    for copy in swaps:
        copy.wait()

    count = dealt.shape[1]
    lane = lax.broadcasted_iota(jnp.int32, (SUBLANES, LANES), 1)
    for col in range(cols):
        here = pl.ds(col * LANES, LANES)
        for kind in range(3):
            stage[kind, col] = state[kind, :, here]
        stage[3, col] = resting[:, here].astype(jnp.float32) / 100.0
        for k in range(count):
            every = pl.ds(k, SUBLANES, stride=count)
            height, east = stage[0, col, every], stage[1, col, every]
            rest = stage[3, col, every]
            dealt[0, k, :, here] = height
            dealt[1, k, :, here] = east
            dealt[2, k, :, here] = stage[2, col, every]
            depth[k, :, here] = rest
            flux[k, :, here] = (rest + height) * east

    def step(_, carry):
        for col in range(cols):
            advance(dealt, flux, depth, middle, flux_mid, None, time_step, col, lane)
        for col in range(cols):
            advance(middle, flux_mid, depth, dealt, flux, dealt, 0.5 * time_step, col, lane)
        return carry

    lax.fori_loop(0, STEPS * CYCLES, step, 0)
    for col in range(cols):
        here = pl.ds(col * LANES, LANES)
        for k in range(count):
            for kind in range(3):
                stage[kind, col, pl.ds(k, SUBLANES, stride=count)] = dealt[kind, k, :, here]

    def piece(kind, j, r):
        return stage.at[
            kind,
            lax.rem(j, cols),
            pl.ds(pl.multiple_of(r * tile_rows + j // cols * part, SUBLANES), part),
        ]

    def spread_copy(kind, other):
        j, r = other // rows_axis, lax.rem(other, rows_axis)
        return pltpu.make_async_remote_copy(
            src_ref=piece(kind, j, r), dst_ref=held[kind].at[me],
            send_sem=spread_send.at[kind, other], recv_sem=spread_recv.at[kind],
            device_id=(j, r), device_id_type=MESH,
        )

    half = devices // 2
    side, seat = me // half, lax.rem(me, half)
    far, near = (1 - side) * half, side * half
    kinds = state.shape[0]

    for kind in range(kinds):
        spread_copy(kind, far + seat).start()

        def start_spread(k, carry, kind=kind):
            there = lax.rem(seat + k, half)
            spread_copy(kind, far + there).start()
            spread_copy(kind, near + there).start()
            return carry

        lax.fori_loop(1, half, start_spread, 0)
        pltpu.make_async_copy(
            piece(kind, group, row_no), held[kind].at[me], spread_recv.at[kind]
        ).start()

    own_lists.wait()

    def compose(m, carry):
        source = m
        for cycle_no in reversed(range(lists.shape[1])):
            for section_no in reversed(range(lists.shape[0])):
                source = lists[section_no, cycle_no, source]
        sources[m] = source
        return carry

    lax.fori_loop(0, sources.shape[0], compose, 0)

    def place(kind):
        return out.at[
            :,
            kind,
            pl.ds(pl.multiple_of(group // cols * part, SUBLANES), part),
            pl.ds(pl.multiple_of(lax.rem(group, cols) * LANES, LANES), LANES),
        ]

    def back_copy(kind, other):
        return pltpu.make_async_remote_copy(
            src_ref=picked[kind].at[pl.ds(other * local, local)], dst_ref=place(kind),
            send_sem=back_send.at[kind, other], recv_sem=back_recv.at[kind],
            device_id=(other, row_no), device_id_type=MESH,
        )

    back_half = members_axis // 2
    back_side, back_seat = group // back_half, lax.rem(group, back_half)
    back_far, back_near = (1 - back_side) * back_half, back_side * back_half

    for kind in range(kinds):
        pltpu.make_async_copy(held[kind], held[kind], spread_recv.at[kind]).wait()
        for m in range(sources.shape[0]):
            picked[kind][m] = held[kind][sources[m]]
        back_copy(kind, back_far + back_seat).start()

        def start_back(k, carry, kind=kind):
            there = lax.rem(back_seat + k, back_half)
            back_copy(kind, back_far + there).start()
            back_copy(kind, back_near + there).start()
            return carry

        lax.fori_loop(1, back_half, start_back, 0)
        pltpu.make_async_copy(
            picked[kind].at[pl.ds(group * local, local)], place(kind), back_recv.at[kind]
        ).start()

    for kind in range(kinds):

        def end_spread(k, carry, kind=kind):
            spread_copy(kind, lax.rem(me + k, devices)).wait_send()
            return carry

        lax.fori_loop(1, devices, end_spread, 0)

        def end_back(k, carry, kind=kind):
            back_copy(kind, lax.rem(group + k, members_axis)).wait_send()
            return carry

        lax.fori_loop(1, members_axis, end_back, 0)
    for kind in range(kinds):
        pltpu.make_async_copy(out.at[:, kind], out.at[:, kind], back_recv.at[kind]).wait()


def fast_body(members_axis, rows_axis, fields, bathymetry, copy_lists):
    local, kinds, tile_rows, width = fields.shape
    rows = tile_rows * rows_axis
    count = rows // SUBLANES
    part = tile_rows // (members_axis // (width // LANES))
    f32 = jnp.float32
    dma = pltpu.SemaphoreType.DMA
    return pl.pallas_call(
        functools.partial(kernel, members_axis, rows_axis),
        out_shape=jax.ShapeDtypeStruct(fields.shape, f32),
        in_specs=[
            pl.BlockSpec(memory_space=pltpu.HBM),
            pl.BlockSpec(memory_space=pltpu.HBM),
            pl.BlockSpec(memory_space=pltpu.HBM),
        ],
        out_specs=pl.BlockSpec(memory_space=pltpu.VMEM),
        scratch_shapes=[
            pltpu.VMEM((kinds, rows, width), f32),
            pltpu.VMEM((kinds + 1, width // LANES, rows, LANES), f32),
            pltpu.VMEM((kinds, count, SUBLANES, width), f32),
            pltpu.VMEM((kinds, count, SUBLANES, width), f32),
            pltpu.VMEM((count, SUBLANES, width), f32),
            pltpu.VMEM((count, SUBLANES, width), f32),
            pltpu.VMEM((rows, width), jnp.int32),
            pltpu.VMEM((count, SUBLANES, width), f32),
            [pltpu.VMEM((members_axis * local, part, LANES), f32)] * kinds,
            [pltpu.VMEM((members_axis * local, part, LANES), f32)] * kinds,
            pltpu.SMEM((copy_lists.shape[1], copy_lists.shape[0], copy_lists.shape[2]), jnp.int32),
            pltpu.SMEM((members_axis * local,), jnp.int32),
            dma((3,)),
            dma((2 * rows_axis,)),
            dma((2 * rows_axis,)),
            dma((kinds, members_axis * rows_axis)),
            dma((kinds,)),
            dma((kinds, members_axis)),
            dma((kinds,)),
        ],
        compiler_params=pltpu.CompilerParams(
            collective_id=0, has_side_effects=True
        ),
    )(fields, bathymetry, jnp.swapaxes(copy_lists, 0, 1))


def solution(mesh):
    members_axis, rows_axis = mesh.shape["member"], mesh.shape["row"]
    placed = (P("member", None, "row", None), P("row", None), P())

    def body(fields, bathymetry, copy_lists):
        local, _, tile_rows, width = fields.shape
        cols = width // LANES
        splits = max(members_axis // cols, 1)
        fits = (
            local == rows_axis
            and width % LANES == 0
            and members_axis % cols == 0
            and members_axis % 2 == 0
            and tile_rows % (splits * SUBLANES) == 0
        )
        if fits:
            return fast_body(members_axis, rows_axis, fields, bathymetry, copy_lists)
        return general_body(fields, bathymetry, copy_lists)

    return jax.shard_map(
        body, mesh=mesh, in_specs=placed, out_specs=P("member", None, "row", None), check_vma=False
    )
```

```python
import functools

import jax
import jax.numpy as jnp
from jax import lax
from jax.experimental import pallas as pl
from jax.experimental.pallas import tpu as pltpu
from jax.sharding import PartitionSpec as P

STEPS = 4
CYCLES = 3


gravity = 2.0
coriolis = 0.1
friction = 0.02
time_step = 0.25

LANES = 128
SUBLANES = 8
MESH = pl.DeviceIdType.MESH


def extended(x, sides, width):
    for axis, dim in sides:
        devices, length = (lax.axis_size(axis), x.shape[dim])
        up = [(i, (i + 1) % devices) for i in range(devices)]
        down = [(j, i) for i, j in up]
        last = lax.slice_in_dim(x, length - width, length, axis=dim)
        leading = lax.slice_in_dim(x, 0, width, axis=dim)
        before = lax.ppermute(last, axis, up)
        after = lax.ppermute(leading, axis, down)
        x = jnp.concatenate([before, x, after], axis=dim)
    return x


def rates(padded, depth_pad):
    height = padded[:, 0]
    east = padded[:, 1]
    north = padded[:, 2]
    column = depth_pad + height
    flux_x = column * east
    flux_y = column * north
    diff_x = (jnp.roll(flux_x, -1, -1) - jnp.roll(flux_x, 1, -1))[:, 1:-1]
    diff_y = flux_y[:, 2:] - flux_y[:, :-2]
    rate_h = -0.5 * (diff_x + diff_y)
    slope_x = (jnp.roll(height, -1, -1) - jnp.roll(height, 1, -1))[:, 1:-1]
    slope_y = height[:, 2:] - height[:, :-2]
    east_mid = east[:, 1:-1]
    north_mid = north[:, 1:-1]
    rate_u = -0.5 * gravity * slope_x + coriolis * north_mid - friction * east_mid
    rate_v = -0.5 * gravity * slope_y - coriolis * east_mid - friction * north_mid
    return jnp.stack([rate_h, rate_u, rate_v], 1)


def trim_depth(depth_full, width):
    offset = 2 * STEPS - width
    total = depth_full.shape[0]
    return depth_full[offset : total - offset]


def general_body(fields, bathymetry, copy_lists):
    depth_ext = extended(bathymetry, (("row", 0),), 2 * STEPS)
    depth_full = depth_ext.astype(jnp.float32) / 100.0
    current = fields
    for _ in range(CYCLES):
        padded = extended(current, (("row", 2),), 2 * STEPS)
        for step_no in range(STEPS):
            width = 2 * (STEPS - step_no)
            first_rate = rates(padded, trim_depth(depth_full, width))
            rows_now = padded.shape[2]
            middle = padded[:, :, 1 : rows_now - 1] + time_step * first_rate
            second_rate = rates(middle, trim_depth(depth_full, width - 1))
            rows_mid = first_rate.shape[2]
            padded = padded[:, :, 2 : rows_now - 2] + 0.5 * time_step * (
                first_rate[:, :, 1 : rows_mid - 1] + second_rate
            )
        current = padded
    sources = jnp.arange(copy_lists.shape[2], dtype=jnp.int32)
    for cycle_no in reversed(range(copy_lists.shape[0])):
        for section_no in reversed(range(copy_lists.shape[1])):
            sources = jnp.take(copy_lists[cycle_no, section_no], sources)
    spread = lax.all_to_all(current, "member", split_axis=3, concat_axis=0, tiled=True)
    return lax.all_to_all(
        jnp.take(spread, sources, axis=0), "member", split_axis=0, concat_axis=3, tiled=True
    )


def advance(state, flux, depth, target, target_flux, base, scale, col, lane):
    cols = state.shape[-1] // LANES
    count = state.shape[1]
    here = pl.ds(col * LANES, LANES)
    left = pl.ds((col - 1) % cols * LANES, LANES)
    right = pl.ds((col + 1) % cols * LANES, LANES)
    first_lane, last_lane = lane == 0, lane == LANES - 1

    def slope_east(ref, k):
        own = ref[k, :, here]
        after = pltpu.roll(jnp.where(first_lane, ref[k, :, right], own), LANES - 1, 1)
        before = pltpu.roll(jnp.where(last_lane, ref[k, :, left], own), 1, 1)
        return after - before

    def slope_north(tiles, k):
        after = tiles[k + 1] if k + 1 < count else pltpu.roll(tiles[0], SUBLANES - 1, 0)
        before = tiles[k - 1] if k > 0 else pltpu.roll(tiles[count - 1], 1, 0)
        return after - before

    keep = 1.0 if base is None else 0.5
    drag = keep - scale * friction
    turn = scale * coriolis
    push = 0.5 * gravity * scale
    heights = [state[0, k, :, here] for k in range(count)]
    norths = [state[2, k, :, here] for k in range(count)]
    rests = [depth[k, :, here] for k in range(count)]
    fluxes = [(rests[k] + heights[k]) * norths[k] for k in range(count)]
    for k in range(count):
        height, north, east = heights[k], norths[k], state[1, k, :, here]
        spread_out = slope_east(flux, k) + slope_north(fluxes, k)
        new_h = (height if base is None else 0.5 * height) - (0.5 * scale) * spread_out
        new_u = drag * east + turn * north - push * slope_east(state.at[0], k)
        new_v = drag * north - turn * east - push * slope_north(heights, k)
        if base is not None:
            new_h = new_h + 0.5 * base[0, k, :, here]
            new_u = new_u + 0.5 * base[1, k, :, here]
            new_v = new_v + 0.5 * base[2, k, :, here]
        target[0, k, :, here] = new_h
        target[1, k, :, here] = new_u
        target[2, k, :, here] = new_v
        target_flux[k, :, here] = (rests[k] + new_h) * new_u


def kernel(
    members_axis, rows_axis, fields, bathymetry, lists_in, out,
    state, stage, dealt, middle, flux, flux_mid, resting, depth, packed, held, picked, landed,
    lists, sources,
    load_sem, swap_send, swap_recv, spread_send, spread_recv, back_send, back_recv,
):
    group, row_no = lax.axis_index("member"), lax.axis_index("row")
    devices = members_axis * rows_axis
    me = group * rows_axis + row_no
    tile_rows, width = fields.shape[2], fields.shape[3]
    rows = tile_rows * rows_axis
    cols = width // LANES
    local = fields.shape[0]
    own_rows = pl.ds(pl.multiple_of(row_no * tile_rows, SUBLANES), tile_rows)

    own_fields = pltpu.make_async_copy(fields.at[row_no], state.at[:, own_rows], load_sem.at[0])
    own_depth = pltpu.make_async_copy(bathymetry, resting.at[own_rows], load_sem.at[1])
    own_lists = pltpu.make_async_copy(lists_in, lists, load_sem.at[2])
    own_fields.start()
    own_depth.start()
    own_lists.start()

    barrier = pltpu.get_barrier_semaphore()

    def greet(k, carry):
        other = lax.rem(me + k, devices)
        pl.semaphore_signal(
            barrier, inc=1, device_id=(other // rows_axis, lax.rem(other, rows_axis)),
            device_id_type=MESH,
        )
        return carry

    lax.fori_loop(1, devices, greet, 0)
    pl.semaphore_wait(barrier, devices - 1)

    swaps = []
    for k in range(1, rows_axis):
        other = lax.rem(row_no + k, rows_axis)
        for n, (src, dst) in enumerate(
            ((bathymetry, resting.at[own_rows]), (fields.at[other], state.at[:, own_rows]))
        ):
            copy = pltpu.make_async_remote_copy(
                src_ref=src, dst_ref=dst,
                send_sem=swap_send.at[2 * k + n], recv_sem=swap_recv.at[2 * k + n],
                device_id=(group, other), device_id_type=MESH,
            )
            copy.start()
            swaps.append(copy)
    own_fields.wait()
    own_depth.wait()
    for copy in swaps:
        copy.wait()

    count = dealt.shape[1]
    lane = lax.broadcasted_iota(jnp.int32, (SUBLANES, LANES), 1)
    for col in range(cols):
        here = pl.ds(col * LANES, LANES)
        for kind in range(3):
            stage[kind, col] = state[kind, :, here]
        stage[3, col] = resting[:, here].astype(jnp.float32) / 100.0
        for k in range(count):
            every = pl.ds(k, SUBLANES, stride=count)
            height, east = stage[0, col, every], stage[1, col, every]
            rest = stage[3, col, every]
            dealt[0, k, :, here] = height
            dealt[1, k, :, here] = east
            dealt[2, k, :, here] = stage[2, col, every]
            depth[k, :, here] = rest
            flux[k, :, here] = (rest + height) * east

    def step(_, carry):
        for col in range(cols):
            advance(dealt, flux, depth, middle, flux_mid, None, time_step, col, lane)
        for col in range(cols):
            advance(middle, flux_mid, depth, dealt, flux, dealt, 0.5 * time_step, col, lane)
        return carry

    lax.fori_loop(0, STEPS * CYCLES, step, 0)
    for col in range(cols):
        here = pl.ds(col * LANES, LANES)
        for k in range(count):
            for kind in range(3):
                stage[kind, col, pl.ds(k, SUBLANES, stride=count)] = dealt[kind, k, :, here]
        for k in range(count):
            for kind in range(3):
                packed[col, k, kind] = stage[kind, col, pl.ds(k * SUBLANES, SUBLANES)]

    def piece(j, r):
        return packed.at[lax.rem(j, cols), r * (tile_rows // SUBLANES) + j // cols]

    def spread_copy(other):
        j, r = other // rows_axis, lax.rem(other, rows_axis)
        return pltpu.make_async_remote_copy(
            src_ref=piece(j, r), dst_ref=held.at[me],
            send_sem=spread_send.at[other], recv_sem=spread_recv,
            device_id=(j, r), device_id_type=MESH,
        )

    half = devices // 2
    side, seat = me // half, lax.rem(me, half)
    far, near = (1 - side) * half, side * half

    spread_copy(far + seat).start()

    def start_spread(k, carry):
        there = lax.rem(seat + k, half)
        spread_copy(far + there).start()
        spread_copy(near + there).start()
        return carry

    lax.fori_loop(1, half, start_spread, 0)
    pltpu.make_async_copy(piece(group, row_no), held.at[me], spread_recv).start()

    own_lists.wait()

    def compose(m, carry):
        source = m
        for cycle_no in reversed(range(lists.shape[1])):
            for section_no in reversed(range(lists.shape[0])):
                source = lists[section_no, cycle_no, source]
        sources[m] = source
        return carry

    lax.fori_loop(0, sources.shape[0], compose, 0)

    def back_copy(other):
        return pltpu.make_async_remote_copy(
            src_ref=picked.at[other], dst_ref=landed.at[group],
            send_sem=back_send.at[other], recv_sem=back_recv,
            device_id=(other, row_no), device_id_type=MESH,
        )

    back_half = members_axis // 2
    back_side, back_seat = group // back_half, lax.rem(group, back_half)
    back_far, back_near = (1 - back_side) * back_half, back_side * back_half

    pltpu.make_async_copy(held, held, spread_recv).wait()
    for m in range(sources.shape[0]):
        picked[m // local, m % local] = held[sources[m]]
    back_copy(back_far + back_seat).start()

    def start_back(k, carry):
        there = lax.rem(back_seat + k, back_half)
        back_copy(back_far + there).start()
        back_copy(back_near + there).start()
        return carry

    lax.fori_loop(1, back_half, start_back, 0)
    pltpu.make_async_copy(picked.at[group], landed.at[group], back_recv).start()

    def end_spread(k, carry):
        spread_copy(lax.rem(me + k, devices)).wait_send()
        return carry

    lax.fori_loop(1, devices, end_spread, 0)

    def end_back(k, carry):
        back_copy(lax.rem(group + k, members_axis)).wait_send()
        return carry

    lax.fori_loop(1, members_axis, end_back, 0)
    pltpu.make_async_copy(landed, landed, back_recv).wait()
    for j in range(members_axis):
        tile = pl.ds(j // cols * SUBLANES, SUBLANES), pl.ds(j % cols * LANES, LANES)
        for m in range(local):
            for kind in range(3):
                out[m, kind, tile[0], tile[1]] = landed[j, m, kind]


def fast_body(members_axis, rows_axis, fields, bathymetry, copy_lists):
    local, kinds, tile_rows, width = fields.shape
    rows = tile_rows * rows_axis
    count = rows // SUBLANES
    f32 = jnp.float32
    dma = pltpu.SemaphoreType.DMA
    return pl.pallas_call(
        functools.partial(kernel, members_axis, rows_axis),
        out_shape=jax.ShapeDtypeStruct(fields.shape, f32),
        in_specs=[
            pl.BlockSpec(memory_space=pltpu.HBM),
            pl.BlockSpec(memory_space=pltpu.HBM),
            pl.BlockSpec(memory_space=pltpu.HBM),
        ],
        out_specs=pl.BlockSpec(memory_space=pltpu.VMEM),
        scratch_shapes=[
            pltpu.VMEM((kinds, rows, width), f32),
            pltpu.VMEM((kinds + 1, width // LANES, rows, LANES), f32),
            pltpu.VMEM((kinds, count, SUBLANES, width), f32),
            pltpu.VMEM((kinds, count, SUBLANES, width), f32),
            pltpu.VMEM((count, SUBLANES, width), f32),
            pltpu.VMEM((count, SUBLANES, width), f32),
            pltpu.VMEM((rows, width), jnp.int32),
            pltpu.VMEM((count, SUBLANES, width), f32),
            pltpu.VMEM((width // LANES, count, kinds, SUBLANES, LANES), f32),
            pltpu.VMEM((members_axis * local, kinds, SUBLANES, LANES), f32),
            pltpu.VMEM((members_axis, local, kinds, SUBLANES, LANES), f32),
            pltpu.VMEM((members_axis, local, kinds, SUBLANES, LANES), f32),
            pltpu.SMEM((copy_lists.shape[1], copy_lists.shape[0], copy_lists.shape[2]), jnp.int32),
            pltpu.SMEM((members_axis * local,), jnp.int32),
            dma((3,)),
            dma((2 * rows_axis,)),
            dma((2 * rows_axis,)),
            dma((members_axis * rows_axis,)),
            dma,
            dma((members_axis,)),
            dma,
        ],
        compiler_params=pltpu.CompilerParams(
            collective_id=0, has_side_effects=True
        ),
    )(fields, bathymetry, jnp.swapaxes(copy_lists, 0, 1))


def solution(mesh):
    members_axis, rows_axis = mesh.shape["member"], mesh.shape["row"]
    placed = (P("member", None, "row", None), P("row", None), P())

    def body(fields, bathymetry, copy_lists):
        local, _, tile_rows, width = fields.shape
        cols = width // LANES
        splits = max(members_axis // cols, 1)
        fits = (
            local == rows_axis
            and width % LANES == 0
            and members_axis % cols == 0
            and members_axis % 2 == 0
            and tile_rows == splits * SUBLANES
        )
        if fits:
            return fast_body(members_axis, rows_axis, fields, bathymetry, copy_lists)
        return general_body(fields, bathymetry, copy_lists)

    return jax.shard_map(
        body, mesh=mesh, in_specs=placed, out_specs=P("member", None, "row", None), check_vma=False
    )
```

```python
import functools

import jax
import jax.numpy as jnp
from jax import lax
from jax.experimental import pallas as pl
from jax.experimental.pallas import tpu as pltpu
from jax.sharding import PartitionSpec as P

STEPS = 4
CYCLES = 3


gravity = 2.0
coriolis = 0.1
friction = 0.02
time_step = 0.25

LANES = 128
SUBLANES = 8
MESH = pl.DeviceIdType.MESH
CHUNKS = 2


def extended(x, sides, width):
    for axis, dim in sides:
        devices, length = (lax.axis_size(axis), x.shape[dim])
        up = [(i, (i + 1) % devices) for i in range(devices)]
        down = [(j, i) for i, j in up]
        last = lax.slice_in_dim(x, length - width, length, axis=dim)
        leading = lax.slice_in_dim(x, 0, width, axis=dim)
        before = lax.ppermute(last, axis, up)
        after = lax.ppermute(leading, axis, down)
        x = jnp.concatenate([before, x, after], axis=dim)
    return x


def rates(padded, depth_pad):
    height = padded[:, 0]
    east = padded[:, 1]
    north = padded[:, 2]
    column = depth_pad + height
    flux_x = column * east
    flux_y = column * north
    diff_x = (jnp.roll(flux_x, -1, -1) - jnp.roll(flux_x, 1, -1))[:, 1:-1]
    diff_y = flux_y[:, 2:] - flux_y[:, :-2]
    rate_h = -0.5 * (diff_x + diff_y)
    slope_x = (jnp.roll(height, -1, -1) - jnp.roll(height, 1, -1))[:, 1:-1]
    slope_y = height[:, 2:] - height[:, :-2]
    east_mid = east[:, 1:-1]
    north_mid = north[:, 1:-1]
    rate_u = -0.5 * gravity * slope_x + coriolis * north_mid - friction * east_mid
    rate_v = -0.5 * gravity * slope_y - coriolis * east_mid - friction * north_mid
    return jnp.stack([rate_h, rate_u, rate_v], 1)


def trim_depth(depth_full, width):
    offset = 2 * STEPS - width
    total = depth_full.shape[0]
    return depth_full[offset : total - offset]


def general_body(fields, bathymetry, copy_lists):
    depth_ext = extended(bathymetry, (("row", 0),), 2 * STEPS)
    depth_full = depth_ext.astype(jnp.float32) / 100.0
    current = fields
    for _ in range(CYCLES):
        padded = extended(current, (("row", 2),), 2 * STEPS)
        for step_no in range(STEPS):
            width = 2 * (STEPS - step_no)
            first_rate = rates(padded, trim_depth(depth_full, width))
            rows_now = padded.shape[2]
            middle = padded[:, :, 1 : rows_now - 1] + time_step * first_rate
            second_rate = rates(middle, trim_depth(depth_full, width - 1))
            rows_mid = first_rate.shape[2]
            padded = padded[:, :, 2 : rows_now - 2] + 0.5 * time_step * (
                first_rate[:, :, 1 : rows_mid - 1] + second_rate
            )
        current = padded
    sources = jnp.arange(copy_lists.shape[2], dtype=jnp.int32)
    for cycle_no in reversed(range(copy_lists.shape[0])):
        for section_no in reversed(range(copy_lists.shape[1])):
            sources = jnp.take(copy_lists[cycle_no, section_no], sources)
    spread = lax.all_to_all(current, "member", split_axis=3, concat_axis=0, tiled=True)
    return lax.all_to_all(
        jnp.take(spread, sources, axis=0), "member", split_axis=0, concat_axis=3, tiled=True
    )


def advance(state, flux, depth, target, target_flux, base, scale, col, lane):
    cols = state.shape[-1] // LANES
    count = state.shape[1]
    here = pl.ds(col * LANES, LANES)
    left = pl.ds((col - 1) % cols * LANES, LANES)
    right = pl.ds((col + 1) % cols * LANES, LANES)
    first_lane, last_lane = lane == 0, lane == LANES - 1

    def slope_east(ref, k):
        own = ref[k, :, here]
        after = pltpu.roll(jnp.where(first_lane, ref[k, :, right], own), LANES - 1, 1)
        before = pltpu.roll(jnp.where(last_lane, ref[k, :, left], own), 1, 1)
        return after - before

    def slope_north(tiles, k):
        after = tiles[k + 1] if k + 1 < count else pltpu.roll(tiles[0], SUBLANES - 1, 0)
        before = tiles[k - 1] if k > 0 else pltpu.roll(tiles[count - 1], 1, 0)
        return after - before

    keep = 1.0 if base is None else 0.5
    drag = keep - scale * friction
    turn = scale * coriolis
    push = 0.5 * gravity * scale
    heights = [state[0, k, :, here] for k in range(count)]
    norths = [state[2, k, :, here] for k in range(count)]
    rests = [depth[k, :, here] for k in range(count)]
    fluxes = [(rests[k] + heights[k]) * norths[k] for k in range(count)]
    for k in range(count):
        height, north, east = heights[k], norths[k], state[1, k, :, here]
        spread_out = slope_east(flux, k) + slope_north(fluxes, k)
        new_h = (height if base is None else 0.5 * height) - (0.5 * scale) * spread_out
        new_u = drag * east + turn * north - push * slope_east(state.at[0], k)
        new_v = drag * north - turn * east - push * slope_north(heights, k)
        if base is not None:
            new_h = new_h + 0.5 * base[0, k, :, here]
            new_u = new_u + 0.5 * base[1, k, :, here]
            new_v = new_v + 0.5 * base[2, k, :, here]
        target[0, k, :, here] = new_h
        target[1, k, :, here] = new_u
        target[2, k, :, here] = new_v
        target_flux[k, :, here] = (rests[k] + new_h) * new_u


def kernel(
    members_axis, rows_axis, fields, bathymetry, lists_in, out,
    state, stage, dealt, deep, work, middle, flux, flux_mid, resting, depth, sent, held, picked,
    lists, sources,
    load_sem, swap_send, swap_recv, spread_send, spread_recv, back_send, back_recv,
):
    group, row_no = lax.axis_index("member"), lax.axis_index("row")
    devices = members_axis * rows_axis
    me = group * rows_axis + row_no
    tile_rows, width = fields.shape[2], fields.shape[3]
    rows = tile_rows * rows_axis
    cols = width // LANES
    local = fields.shape[0]
    own_rows = pl.ds(pl.multiple_of(row_no * tile_rows, SUBLANES), tile_rows)

    own_fields = pltpu.make_async_copy(fields.at[row_no], state.at[:, own_rows], load_sem.at[0])
    own_depth = pltpu.make_async_copy(bathymetry, resting.at[own_rows], load_sem.at[1])
    own_lists = pltpu.make_async_copy(lists_in, lists, load_sem.at[2])
    own_fields.start()
    own_depth.start()
    own_lists.start()

    barrier = pltpu.get_barrier_semaphore()

    def greet(k, carry):
        other = lax.rem(me + k, devices)
        pl.semaphore_signal(
            barrier, inc=1, device_id=(other // rows_axis, lax.rem(other, rows_axis)),
            device_id_type=MESH,
        )
        return carry

    lax.fori_loop(1, devices, greet, 0)
    pl.semaphore_wait(barrier, devices - 1)

    swaps = []
    for k in range(1, rows_axis):
        other = lax.rem(row_no + k, rows_axis)
        for n, (src, dst) in enumerate(
            ((bathymetry, resting.at[own_rows]), (fields.at[other], state.at[:, own_rows]))
        ):
            copy = pltpu.make_async_remote_copy(
                src_ref=src, dst_ref=dst,
                send_sem=swap_send.at[2 * k + n], recv_sem=swap_recv.at[2 * k + n],
                device_id=(group, other), device_id_type=MESH,
            )
            copy.start()
            swaps.append(copy)
    own_fields.wait()
    own_depth.wait()
    for copy in swaps:
        copy.wait()

    count = dealt.shape[1]
    lane = lax.broadcasted_iota(jnp.int32, (SUBLANES, LANES), 1)
    for col in range(cols):
        here = pl.ds(col * LANES, LANES)
        for kind in range(3):
            stage[kind, col] = state[kind, :, here]
        stage[3, col] = resting[:, here].astype(jnp.float32) / 100.0
        for k in range(count):
            every = pl.ds(k, SUBLANES, stride=count)
            for kind in range(3):
                dealt[kind, k, :, here] = stage[kind, col, every]
            deep[k, :, here] = stage[3, col, every]

    own_lists.wait()
    steps = STEPS * CYCLES
    members = sources.shape[0]
    share = -(-members // steps)

    def compose(m):
        source = m
        for cycle_no in reversed(range(lists.shape[1])):
            for section_no in reversed(range(lists.shape[0])):
                source = lists[section_no, cycle_no, source]
        sources[m] = source

    chunk_cols = cols // CHUNKS

    def forecast(q):
        first = q * chunk_cols
        follows = lane < LANES // 2
        for col in range(chunk_cols + 1):
            here = pl.ds(col * LANES, LANES)
            after = pl.ds((first + col) % cols * LANES, LANES)
            before = pl.ds((first - 1) % cols * LANES, LANES)

            def taken(ref, k, col=col, after=after, before=before):
                if col < chunk_cols:
                    return ref[k, :, after]
                return jnp.where(follows, ref[k, :, after], ref[k, :, before])

            for k in range(count):
                height, east, north = [taken(dealt.at[kind], k) for kind in range(3)]
                rest = taken(deep, k)
                work[0, k, :, here] = height
                work[1, k, :, here] = east
                work[2, k, :, here] = north
                depth[k, :, here] = rest
                flux[k, :, here] = (rest + height) * east

        def step(i, carry):
            if q == 0:
                for n in range(share):
                    compose(jnp.minimum(i * share + n, members - 1))
            for col in range(chunk_cols + 1):
                advance(work, flux, depth, middle, flux_mid, None, time_step, col, lane)
            for col in range(chunk_cols + 1):
                advance(middle, flux_mid, depth, work, flux, work, 0.5 * time_step, col, lane)
            return carry

        lax.fori_loop(0, steps, step, 0)
        for col in range(chunk_cols):
            here = pl.ds(col * LANES, LANES)
            for k in range(count):
                for kind in range(3):
                    sent[q][kind, col, pl.ds(k, SUBLANES, stride=count)] = work[kind, k, :, here]

    stages = [(q, kind) for q in range(CHUNKS) for kind in range(3)]

    def core_of(i):
        return sum(stages[i]) % rows_axis

    def spread_copy(i, j):
        q, kind = stages[i]
        src = sent[q].at[
            kind,
            lax.rem(j, chunk_cols),
            pl.ds(pl.multiple_of(j // chunk_cols * SUBLANES, SUBLANES), SUBLANES),
        ]
        return src, pltpu.make_async_remote_copy(
            src_ref=src, dst_ref=held[i].at[me],
            send_sem=spread_send.at[i, j], recv_sem=spread_recv.at[i],
            device_id=(j, core_of(i)), device_id_type=MESH,
        )

    half = members_axis // 2
    side, seat = group // half, lax.rem(group, half)
    far, near = (1 - side) * half, side * half

    def send_all(copy, own_is_local, own_dst, own_sem):
        copy(far + seat)[1].start()

        def start(k, carry):
            there = lax.rem(seat + k, half)
            copy(far + there)[1].start()
            copy(near + there)[1].start()
            return carry

        lax.fori_loop(1, half, start, 0)
        src, remote = copy(group)

        @pl.when(own_is_local)
        def _():
            pltpu.make_async_copy(src, own_dst, own_sem).start()

        @pl.when(jnp.logical_not(own_is_local))
        def _():
            remote.start()

    def end_all(copy, own_is_local):
        def end(k, carry):
            copy(lax.rem(group + k, members_axis))[1].wait_send()
            return carry

        lax.fori_loop(1, members_axis, end, 0)

        @pl.when(jnp.logical_not(own_is_local))
        def _():
            copy(group)[1].wait_send()

    my_row = group // chunk_cols * SUBLANES
    home = my_row // tile_rows

    def place(i):
        q, kind = stages[i]
        return out.at[
            :,
            kind,
            pl.ds(pl.multiple_of(lax.rem(my_row, tile_rows), SUBLANES), SUBLANES),
            pl.ds(
                pl.multiple_of((q * chunk_cols + lax.rem(group, chunk_cols)) * LANES, LANES),
                LANES,
            ),
        ]

    def back_copy(i, other):
        src = picked[i].at[pl.ds(other * local, local)]
        return src, pltpu.make_async_remote_copy(
            src_ref=src, dst_ref=place(i),
            send_sem=back_send.at[i, other], recv_sem=back_recv.at[i],
            device_id=(other, home), device_id_type=MESH,
        )

    for q in range(CHUNKS):
        forecast(q)
        for i in range(3 * q, 3 * q + 3):
            send_all(
                functools.partial(spread_copy, i),
                row_no == core_of(i), held[i].at[me], spread_recv.at[i],
            )

    for i in range(len(stages)):

        @pl.when(row_no == core_of(i))
        def _(i=i):
            pltpu.make_async_copy(held[i], held[i], spread_recv.at[i]).wait()
            for m in range(members):
                picked[i][m] = held[i][sources[m]]
            send_all(
                functools.partial(back_copy, i), row_no == home, place(i), back_recv.at[i]
            )

    for i, (q, kind) in enumerate(stages):
        end_all(functools.partial(spread_copy, i), row_no == core_of(i))

        @pl.when(row_no == core_of(i))
        def _(i=i):
            end_all(functools.partial(back_copy, i), row_no == home)

    for i, (q, kind) in enumerate(stages):
        landed = out.at[:, kind, :, pl.ds(q * chunk_cols * LANES, chunk_cols * LANES)]
        pltpu.make_async_copy(landed, landed, back_recv.at[i]).wait()


def fast_body(members_axis, rows_axis, fields, bathymetry, copy_lists):
    local, kinds, tile_rows, width = fields.shape
    rows = tile_rows * rows_axis
    count = rows // SUBLANES
    chunk_width = width // CHUNKS + LANES
    members = members_axis * local
    f32 = jnp.float32
    dma = pltpu.SemaphoreType.DMA
    return pl.pallas_call(
        functools.partial(kernel, members_axis, rows_axis),
        out_shape=jax.ShapeDtypeStruct(fields.shape, f32),
        in_specs=[
            pl.BlockSpec(memory_space=pltpu.HBM),
            pl.BlockSpec(memory_space=pltpu.HBM),
            pl.BlockSpec(memory_space=pltpu.HBM),
        ],
        out_specs=pl.BlockSpec(memory_space=pltpu.VMEM),
        scratch_shapes=[
            pltpu.VMEM((kinds, rows, width), f32),
            pltpu.VMEM((kinds + 1, width // LANES, rows, LANES), f32),
            pltpu.VMEM((kinds, count, SUBLANES, width), f32),
            pltpu.VMEM((count, SUBLANES, width), f32),
            pltpu.VMEM((kinds, count, SUBLANES, chunk_width), f32),
            pltpu.VMEM((kinds, count, SUBLANES, chunk_width), f32),
            pltpu.VMEM((count, SUBLANES, chunk_width), f32),
            pltpu.VMEM((count, SUBLANES, chunk_width), f32),
            pltpu.VMEM((rows, width), jnp.int32),
            pltpu.VMEM((count, SUBLANES, chunk_width), f32),
            [pltpu.VMEM((kinds, width // LANES // CHUNKS, rows, LANES), f32)] * CHUNKS,
            [pltpu.VMEM((members, SUBLANES, LANES), f32)] * (CHUNKS * kinds),
            [pltpu.VMEM((members, SUBLANES, LANES), f32)] * (CHUNKS * kinds),
            pltpu.SMEM((copy_lists.shape[1], copy_lists.shape[0], copy_lists.shape[2]), jnp.int32),
            pltpu.SMEM((members,), jnp.int32),
            dma((3,)),
            dma((2 * rows_axis,)),
            dma((2 * rows_axis,)),
            dma((CHUNKS * kinds, members_axis)),
            dma((CHUNKS * kinds,)),
            dma((CHUNKS * kinds, members_axis)),
            dma((CHUNKS * kinds,)),
        ],
        compiler_params=pltpu.CompilerParams(
            collective_id=0, has_side_effects=True
        ),
    )(fields, bathymetry, jnp.swapaxes(copy_lists, 0, 1))


def solution(mesh):
    members_axis, rows_axis = mesh.shape["member"], mesh.shape["row"]
    placed = (P("member", None, "row", None), P("row", None), P())

    def body(fields, bathymetry, copy_lists):
        local, _, tile_rows, width = fields.shape
        chunk_cols = width // (LANES * CHUNKS)
        row_tiles = tile_rows * rows_axis // SUBLANES
        fits = (
            local == rows_axis
            and width % (LANES * CHUNKS) == 0
            and tile_rows % SUBLANES == 0
            and members_axis % 2 == 0
            and members_axis == row_tiles * chunk_cols
            and 2 * STEPS * CYCLES <= LANES // 2
        )
        if fits:
            return fast_body(members_axis, rows_axis, fields, bathymetry, copy_lists)
        return general_body(fields, bathymetry, copy_lists)

    return jax.shard_map(
        body, mesh=mesh, in_specs=placed, out_specs=P("member", None, "row", None), check_vma=False
    )
```

```python
import functools

import jax
import jax.numpy as jnp
from jax import lax
from jax.experimental import pallas as pl
from jax.experimental.pallas import tpu as pltpu
from jax.sharding import PartitionSpec as P

STEPS = 4
CYCLES = 3


gravity = 2.0
coriolis = 0.1
friction = 0.02
time_step = 0.25

LANES = 128
SUBLANES = 8
MESH = pl.DeviceIdType.MESH
CHUNKS = 2


def extended(x, sides, width):
    for axis, dim in sides:
        devices, length = (lax.axis_size(axis), x.shape[dim])
        up = [(i, (i + 1) % devices) for i in range(devices)]
        down = [(j, i) for i, j in up]
        last = lax.slice_in_dim(x, length - width, length, axis=dim)
        leading = lax.slice_in_dim(x, 0, width, axis=dim)
        before = lax.ppermute(last, axis, up)
        after = lax.ppermute(leading, axis, down)
        x = jnp.concatenate([before, x, after], axis=dim)
    return x


def rates(padded, depth_pad):
    height = padded[:, 0]
    east = padded[:, 1]
    north = padded[:, 2]
    column = depth_pad + height
    flux_x = column * east
    flux_y = column * north
    diff_x = (jnp.roll(flux_x, -1, -1) - jnp.roll(flux_x, 1, -1))[:, 1:-1]
    diff_y = flux_y[:, 2:] - flux_y[:, :-2]
    rate_h = -0.5 * (diff_x + diff_y)
    slope_x = (jnp.roll(height, -1, -1) - jnp.roll(height, 1, -1))[:, 1:-1]
    slope_y = height[:, 2:] - height[:, :-2]
    east_mid = east[:, 1:-1]
    north_mid = north[:, 1:-1]
    rate_u = -0.5 * gravity * slope_x + coriolis * north_mid - friction * east_mid
    rate_v = -0.5 * gravity * slope_y - coriolis * east_mid - friction * north_mid
    return jnp.stack([rate_h, rate_u, rate_v], 1)


def trim_depth(depth_full, width):
    offset = 2 * STEPS - width
    total = depth_full.shape[0]
    return depth_full[offset : total - offset]


def general_body(fields, bathymetry, copy_lists):
    depth_ext = extended(bathymetry, (("row", 0),), 2 * STEPS)
    depth_full = depth_ext.astype(jnp.float32) / 100.0
    current = fields
    for _ in range(CYCLES):
        padded = extended(current, (("row", 2),), 2 * STEPS)
        for step_no in range(STEPS):
            width = 2 * (STEPS - step_no)
            first_rate = rates(padded, trim_depth(depth_full, width))
            rows_now = padded.shape[2]
            middle = padded[:, :, 1 : rows_now - 1] + time_step * first_rate
            second_rate = rates(middle, trim_depth(depth_full, width - 1))
            rows_mid = first_rate.shape[2]
            padded = padded[:, :, 2 : rows_now - 2] + 0.5 * time_step * (
                first_rate[:, :, 1 : rows_mid - 1] + second_rate
            )
        current = padded
    sources = jnp.arange(copy_lists.shape[2], dtype=jnp.int32)
    for cycle_no in reversed(range(copy_lists.shape[0])):
        for section_no in reversed(range(copy_lists.shape[1])):
            sources = jnp.take(copy_lists[cycle_no, section_no], sources)
    spread = lax.all_to_all(current, "member", split_axis=3, concat_axis=0, tiled=True)
    return lax.all_to_all(
        jnp.take(spread, sources, axis=0), "member", split_axis=0, concat_axis=3, tiled=True
    )


def advance(state, flux, depth, target, target_flux, base, scale, col, lane):
    cols = state.shape[-1] // LANES
    count = state.shape[1]
    here = pl.ds(col * LANES, LANES)
    left = pl.ds((col - 1) % cols * LANES, LANES)
    right = pl.ds((col + 1) % cols * LANES, LANES)
    first_lane, last_lane = lane == 0, lane == LANES - 1

    def slope_east(ref, k):
        own = ref[k, :, here]
        after = pltpu.roll(jnp.where(first_lane, ref[k, :, right], own), LANES - 1, 1)
        before = pltpu.roll(jnp.where(last_lane, ref[k, :, left], own), 1, 1)
        return after - before

    def slope_north(tiles, k):
        after = tiles[k + 1] if k + 1 < count else pltpu.roll(tiles[0], SUBLANES - 1, 0)
        before = tiles[k - 1] if k > 0 else pltpu.roll(tiles[count - 1], 1, 0)
        return after - before

    keep = 1.0 if base is None else 0.5
    drag = keep - scale * friction
    turn = scale * coriolis
    push = 0.5 * gravity * scale
    heights = [state[0, k, :, here] for k in range(count)]
    norths = [state[2, k, :, here] for k in range(count)]
    rests = [depth[k, :, here] for k in range(count)]
    fluxes = [(rests[k] + heights[k]) * norths[k] for k in range(count)]
    for k in range(count):
        height, north, east = heights[k], norths[k], state[1, k, :, here]
        spread_out = slope_east(flux, k) + slope_north(fluxes, k)
        new_h = (height if base is None else 0.5 * height) - (0.5 * scale) * spread_out
        new_u = drag * east + turn * north - push * slope_east(state.at[0], k)
        new_v = drag * north - turn * east - push * slope_north(heights, k)
        if base is not None:
            new_h = new_h + 0.5 * base[0, k, :, here]
            new_u = new_u + 0.5 * base[1, k, :, here]
            new_v = new_v + 0.5 * base[2, k, :, here]
        target[0, k, :, here] = new_h
        target[1, k, :, here] = new_u
        target[2, k, :, here] = new_v
        target_flux[k, :, here] = (rests[k] + new_h) * new_u


def kernel(
    members_axis, rows_axis, fields, bathymetry, lists_in, out,
    state, stage, dealt, deep, work, middle, flux, flux_mid, resting, depth, sent, held, picked,
    lists, sources,
    load_sem, swap_send, swap_recv, spread_send, spread_recv, back_send, back_recv,
):
    group, row_no = lax.axis_index("member"), lax.axis_index("row")
    devices = members_axis * rows_axis
    me = group * rows_axis + row_no
    tile_rows, width = fields.shape[2], fields.shape[3]
    rows = tile_rows * rows_axis
    cols = width // LANES
    local = fields.shape[0]
    own_rows = pl.ds(pl.multiple_of(row_no * tile_rows, SUBLANES), tile_rows)

    own_fields = pltpu.make_async_copy(fields.at[row_no], state.at[:, own_rows], load_sem.at[0])
    own_depth = pltpu.make_async_copy(bathymetry, resting.at[own_rows], load_sem.at[1])
    own_lists = pltpu.make_async_copy(lists_in, lists, load_sem.at[2])
    own_fields.start()
    own_depth.start()
    own_lists.start()

    barrier = pltpu.get_barrier_semaphore()

    def greet(k, carry):
        other = lax.rem(me + k, devices)
        pl.semaphore_signal(
            barrier, inc=1, device_id=(other // rows_axis, lax.rem(other, rows_axis)),
            device_id_type=MESH,
        )
        return carry

    lax.fori_loop(1, devices, greet, 0)
    pl.semaphore_wait(barrier, devices - 1)

    swaps = []
    for k in range(1, rows_axis):
        other = lax.rem(row_no + k, rows_axis)
        for n, (src, dst) in enumerate(
            ((bathymetry, resting.at[own_rows]), (fields.at[other], state.at[:, own_rows]))
        ):
            copy = pltpu.make_async_remote_copy(
                src_ref=src, dst_ref=dst,
                send_sem=swap_send.at[2 * k + n], recv_sem=swap_recv.at[2 * k + n],
                device_id=(group, other), device_id_type=MESH,
            )
            copy.start()
            swaps.append(copy)
    own_fields.wait()
    own_depth.wait()
    for copy in swaps:
        copy.wait()

    count = dealt.shape[1]
    lane = lax.broadcasted_iota(jnp.int32, (SUBLANES, LANES), 1)
    for col in range(cols):
        here = pl.ds(col * LANES, LANES)
        for kind in range(3):
            stage[kind, col] = state[kind, :, here]
        stage[3, col] = resting[:, here].astype(jnp.float32) / 100.0
        for k in range(count):
            every = pl.ds(k, SUBLANES, stride=count)
            for kind in range(3):
                dealt[kind, k, :, here] = stage[kind, col, every]
            deep[k, :, here] = stage[3, col, every]

    own_lists.wait()
    steps = STEPS * CYCLES
    members = sources.shape[0]
    share = -(-members // steps)

    def compose(m):
        source = m
        for cycle_no in reversed(range(lists.shape[1])):
            for section_no in reversed(range(lists.shape[0])):
                source = lists[section_no, cycle_no, source]
        sources[m] = source

    chunk_cols = cols // CHUNKS

    def forecast(q):
        first = q * chunk_cols
        follows = lane < LANES // 2
        for col in range(chunk_cols + 1):
            here = pl.ds(col * LANES, LANES)
            after = pl.ds((first + col) % cols * LANES, LANES)
            before = pl.ds((first - 1) % cols * LANES, LANES)

            def taken(ref, k, col=col, after=after, before=before):
                if col < chunk_cols:
                    return ref[k, :, after]
                return jnp.where(follows, ref[k, :, after], ref[k, :, before])

            for k in range(count):
                height, east, north = [taken(dealt.at[kind], k) for kind in range(3)]
                rest = taken(deep, k)
                work[0, k, :, here] = height
                work[1, k, :, here] = east
                work[2, k, :, here] = north
                depth[k, :, here] = rest
                flux[k, :, here] = (rest + height) * east

        def step(i, carry):
            if q == 0:
                for n in range(share):
                    compose(jnp.minimum(i * share + n, members - 1))
            for col in range(chunk_cols + 1):
                advance(work, flux, depth, middle, flux_mid, None, time_step, col, lane)
            for col in range(chunk_cols + 1):
                advance(middle, flux_mid, depth, work, flux, work, 0.5 * time_step, col, lane)
            return carry

        lax.fori_loop(0, steps, step, 0)
        for col in range(chunk_cols):
            here = pl.ds(col * LANES, LANES)
            for k in range(count):
                for kind in range(3):
                    sent[q][kind, col, pl.ds(k, SUBLANES, stride=count)] = work[kind, k, :, here]

    def core_of(i):
        return i % rows_axis

    def spread_copy(i, j):
        src = sent[i].at[
            :,
            lax.rem(j, chunk_cols),
            pl.ds(pl.multiple_of(j // chunk_cols * SUBLANES, SUBLANES), SUBLANES),
        ]
        return src, pltpu.make_async_remote_copy(
            src_ref=src, dst_ref=held[i].at[me],
            send_sem=spread_send.at[i, j], recv_sem=spread_recv.at[i],
            device_id=(j, core_of(i)), device_id_type=MESH,
        )

    half = members_axis // 2
    side, seat = group // half, lax.rem(group, half)
    far, near = (1 - side) * half, side * half

    def send_all(copy, own_is_local, own_dst, own_sem):
        copy(far + seat)[1].start()

        def start(k, carry):
            there = lax.rem(seat + k, half)
            copy(far + there)[1].start()
            copy(near + there)[1].start()
            return carry

        lax.fori_loop(1, half, start, 0)
        src, remote = copy(group)

        @pl.when(own_is_local)
        def _():
            pltpu.make_async_copy(src, own_dst, own_sem).start()

        @pl.when(jnp.logical_not(own_is_local))
        def _():
            remote.start()

    def end_all(copy, own_is_local):
        def end(k, carry):
            copy(lax.rem(group + k, members_axis))[1].wait_send()
            return carry

        lax.fori_loop(1, members_axis, end, 0)

        @pl.when(jnp.logical_not(own_is_local))
        def _():
            copy(group)[1].wait_send()

    my_row = group // chunk_cols * SUBLANES
    home = my_row // tile_rows

    def place(i):
        return out.at[
            :,
            :,
            pl.ds(pl.multiple_of(lax.rem(my_row, tile_rows), SUBLANES), SUBLANES),
            pl.ds(
                pl.multiple_of((i * chunk_cols + lax.rem(group, chunk_cols)) * LANES, LANES),
                LANES,
            ),
        ]

    def back_copy(i, other):
        src = picked[i].at[pl.ds(other * local, local)]
        return src, pltpu.make_async_remote_copy(
            src_ref=src, dst_ref=place(i),
            send_sem=back_send.at[i, other], recv_sem=back_recv.at[i],
            device_id=(other, home), device_id_type=MESH,
        )

    for q in range(CHUNKS):
        forecast(q)
        send_all(
            functools.partial(spread_copy, q),
            row_no == core_of(q), held[q].at[me], spread_recv.at[q],
        )

    for i in range(CHUNKS):

        @pl.when(row_no == core_of(i))
        def _(i=i):
            pltpu.make_async_copy(held[i], held[i], spread_recv.at[i]).wait()
            for m in range(members):
                picked[i][m] = held[i][sources[m]]
            send_all(
                functools.partial(back_copy, i), row_no == home, place(i), back_recv.at[i]
            )

    for i in range(CHUNKS):
        end_all(functools.partial(spread_copy, i), row_no == core_of(i))

        @pl.when(row_no == core_of(i))
        def _(i=i):
            end_all(functools.partial(back_copy, i), row_no == home)

    for i in range(CHUNKS):
        landed = out.at[:, :, :, pl.ds(i * chunk_cols * LANES, chunk_cols * LANES)]
        pltpu.make_async_copy(landed, landed, back_recv.at[i]).wait()


def fast_body(members_axis, rows_axis, fields, bathymetry, copy_lists):
    local, kinds, tile_rows, width = fields.shape
    rows = tile_rows * rows_axis
    count = rows // SUBLANES
    chunk_width = width // CHUNKS + LANES
    members = members_axis * local
    f32 = jnp.float32
    dma = pltpu.SemaphoreType.DMA
    return pl.pallas_call(
        functools.partial(kernel, members_axis, rows_axis),
        out_shape=jax.ShapeDtypeStruct(fields.shape, f32),
        in_specs=[
            pl.BlockSpec(memory_space=pltpu.HBM),
            pl.BlockSpec(memory_space=pltpu.HBM),
            pl.BlockSpec(memory_space=pltpu.HBM),
        ],
        out_specs=pl.BlockSpec(memory_space=pltpu.VMEM),
        scratch_shapes=[
            pltpu.VMEM((kinds, rows, width), f32),
            pltpu.VMEM((kinds + 1, width // LANES, rows, LANES), f32),
            pltpu.VMEM((kinds, count, SUBLANES, width), f32),
            pltpu.VMEM((count, SUBLANES, width), f32),
            pltpu.VMEM((kinds, count, SUBLANES, chunk_width), f32),
            pltpu.VMEM((kinds, count, SUBLANES, chunk_width), f32),
            pltpu.VMEM((count, SUBLANES, chunk_width), f32),
            pltpu.VMEM((count, SUBLANES, chunk_width), f32),
            pltpu.VMEM((rows, width), jnp.int32),
            pltpu.VMEM((count, SUBLANES, chunk_width), f32),
            [pltpu.VMEM((kinds, width // LANES // CHUNKS, rows, LANES), f32)] * CHUNKS,
            [pltpu.VMEM((members, kinds, SUBLANES, LANES), f32)] * CHUNKS,
            [pltpu.VMEM((members, kinds, SUBLANES, LANES), f32)] * CHUNKS,
            pltpu.SMEM((copy_lists.shape[1], copy_lists.shape[0], copy_lists.shape[2]), jnp.int32),
            pltpu.SMEM((members,), jnp.int32),
            dma((3,)),
            dma((2 * rows_axis,)),
            dma((2 * rows_axis,)),
            dma((CHUNKS, members_axis)),
            dma((CHUNKS,)),
            dma((CHUNKS, members_axis)),
            dma((CHUNKS,)),
        ],
        compiler_params=pltpu.CompilerParams(
            collective_id=0, has_side_effects=True
        ),
    )(fields, bathymetry, jnp.swapaxes(copy_lists, 0, 1))


def solution(mesh):
    members_axis, rows_axis = mesh.shape["member"], mesh.shape["row"]
    placed = (P("member", None, "row", None), P("row", None), P())

    def body(fields, bathymetry, copy_lists):
        local, _, tile_rows, width = fields.shape
        chunk_cols = width // (LANES * CHUNKS)
        row_tiles = tile_rows * rows_axis // SUBLANES
        fits = (
            local == rows_axis
            and width % (LANES * CHUNKS) == 0
            and tile_rows % SUBLANES == 0
            and members_axis % 2 == 0
            and members_axis == row_tiles * chunk_cols
            and 2 * STEPS * CYCLES <= LANES // 2
        )
        if fits:
            return fast_body(members_axis, rows_axis, fields, bathymetry, copy_lists)
        return general_body(fields, bathymetry, copy_lists)

    return jax.shard_map(
        body, mesh=mesh, in_specs=placed, out_specs=P("member", None, "row", None), check_vma=False
    )
```

```python
import functools

import jax
import jax.numpy as jnp
from jax import lax
from jax.experimental import pallas as pl
from jax.experimental.pallas import tpu as pltpu
from jax.sharding import PartitionSpec as P

STEPS = 4
CYCLES = 3


gravity = 2.0
coriolis = 0.1
friction = 0.02
time_step = 0.25

LANES = 128
SUBLANES = 8
MESH = pl.DeviceIdType.MESH
CHUNKS = 2


def extended(x, sides, width):
    for axis, dim in sides:
        devices, length = (lax.axis_size(axis), x.shape[dim])
        up = [(i, (i + 1) % devices) for i in range(devices)]
        down = [(j, i) for i, j in up]
        last = lax.slice_in_dim(x, length - width, length, axis=dim)
        leading = lax.slice_in_dim(x, 0, width, axis=dim)
        before = lax.ppermute(last, axis, up)
        after = lax.ppermute(leading, axis, down)
        x = jnp.concatenate([before, x, after], axis=dim)
    return x


def rates(padded, depth_pad):
    height = padded[:, 0]
    east = padded[:, 1]
    north = padded[:, 2]
    column = depth_pad + height
    flux_x = column * east
    flux_y = column * north
    diff_x = (jnp.roll(flux_x, -1, -1) - jnp.roll(flux_x, 1, -1))[:, 1:-1]
    diff_y = flux_y[:, 2:] - flux_y[:, :-2]
    rate_h = -0.5 * (diff_x + diff_y)
    slope_x = (jnp.roll(height, -1, -1) - jnp.roll(height, 1, -1))[:, 1:-1]
    slope_y = height[:, 2:] - height[:, :-2]
    east_mid = east[:, 1:-1]
    north_mid = north[:, 1:-1]
    rate_u = -0.5 * gravity * slope_x + coriolis * north_mid - friction * east_mid
    rate_v = -0.5 * gravity * slope_y - coriolis * east_mid - friction * north_mid
    return jnp.stack([rate_h, rate_u, rate_v], 1)


def trim_depth(depth_full, width):
    offset = 2 * STEPS - width
    total = depth_full.shape[0]
    return depth_full[offset : total - offset]


def general_body(fields, bathymetry, copy_lists):
    depth_ext = extended(bathymetry, (("row", 0),), 2 * STEPS)
    depth_full = depth_ext.astype(jnp.float32) / 100.0
    current = fields
    for _ in range(CYCLES):
        padded = extended(current, (("row", 2),), 2 * STEPS)
        for step_no in range(STEPS):
            width = 2 * (STEPS - step_no)
            first_rate = rates(padded, trim_depth(depth_full, width))
            rows_now = padded.shape[2]
            middle = padded[:, :, 1 : rows_now - 1] + time_step * first_rate
            second_rate = rates(middle, trim_depth(depth_full, width - 1))
            rows_mid = first_rate.shape[2]
            padded = padded[:, :, 2 : rows_now - 2] + 0.5 * time_step * (
                first_rate[:, :, 1 : rows_mid - 1] + second_rate
            )
        current = padded
    sources = jnp.arange(copy_lists.shape[2], dtype=jnp.int32)
    for cycle_no in reversed(range(copy_lists.shape[0])):
        for section_no in reversed(range(copy_lists.shape[1])):
            sources = jnp.take(copy_lists[cycle_no, section_no], sources)
    spread = lax.all_to_all(current, "member", split_axis=3, concat_axis=0, tiled=True)
    return lax.all_to_all(
        jnp.take(spread, sources, axis=0), "member", split_axis=0, concat_axis=3, tiled=True
    )


def advance(state, flux, depth, target, target_flux, base, scale, col, lane):
    cols = state.shape[-1] // LANES
    count = state.shape[1]
    here = pl.ds(col * LANES, LANES)
    left = pl.ds((col - 1) % cols * LANES, LANES)
    right = pl.ds((col + 1) % cols * LANES, LANES)
    first_lane, last_lane = lane == 0, lane == LANES - 1

    def slope_east(ref, k):
        own = ref[k, :, here]
        after = pltpu.roll(jnp.where(first_lane, ref[k, :, right], own), LANES - 1, 1)
        before = pltpu.roll(jnp.where(last_lane, ref[k, :, left], own), 1, 1)
        return after - before

    def slope_north(tiles, k):
        after = tiles[k + 1] if k + 1 < count else pltpu.roll(tiles[0], SUBLANES - 1, 0)
        before = tiles[k - 1] if k > 0 else pltpu.roll(tiles[count - 1], 1, 0)
        return after - before

    keep = 1.0 if base is None else 0.5
    drag = keep - scale * friction
    turn = scale * coriolis
    push = 0.5 * gravity * scale
    heights = [state[0, k, :, here] for k in range(count)]
    norths = [state[2, k, :, here] for k in range(count)]
    rests = [depth[k, :, here] for k in range(count)]
    fluxes = [(rests[k] + heights[k]) * norths[k] for k in range(count)]
    for k in range(count):
        height, north, east = heights[k], norths[k], state[1, k, :, here]
        spread_out = slope_east(flux, k) + slope_north(fluxes, k)
        new_h = (height if base is None else 0.5 * height) - (0.5 * scale) * spread_out
        new_u = drag * east + turn * north - push * slope_east(state.at[0], k)
        new_v = drag * north - turn * east - push * slope_north(heights, k)
        if base is not None:
            new_h = new_h + 0.5 * base[0, k, :, here]
            new_u = new_u + 0.5 * base[1, k, :, here]
            new_v = new_v + 0.5 * base[2, k, :, here]
        target[0, k, :, here] = new_h
        target[1, k, :, here] = new_u
        target[2, k, :, here] = new_v
        target_flux[k, :, here] = (rests[k] + new_h) * new_u


def kernel(
    members_axis, rows_axis, fields, bathymetry, lists_in, out,
    state, stage, dealt, deep, work, middle, flux, flux_mid, resting, depth, sent, held, picked,
    lists, sources,
    load_sem, swap_send, swap_recv, spread_send, spread_recv, back_send, back_recv,
):
    group, row_no = lax.axis_index("member"), lax.axis_index("row")
    devices = members_axis * rows_axis
    me = group * rows_axis + row_no
    tile_rows, width = fields.shape[2], fields.shape[3]
    rows = tile_rows * rows_axis
    cols = width // LANES
    local = fields.shape[0]
    own_rows = pl.ds(pl.multiple_of(row_no * tile_rows, SUBLANES), tile_rows)

    own_fields = pltpu.make_async_copy(fields.at[row_no], state.at[:, own_rows], load_sem.at[0])
    own_depth = pltpu.make_async_copy(bathymetry, resting.at[own_rows], load_sem.at[1])
    own_lists = pltpu.make_async_copy(lists_in, lists, load_sem.at[2])
    own_fields.start()
    own_depth.start()
    own_lists.start()

    barrier = pltpu.get_barrier_semaphore()

    def greet(k, carry):
        other = lax.rem(me + k, devices)
        pl.semaphore_signal(
            barrier, inc=1, device_id=(other // rows_axis, lax.rem(other, rows_axis)),
            device_id_type=MESH,
        )
        return carry

    lax.fori_loop(1, devices, greet, 0)
    pl.semaphore_wait(barrier, devices - 1)

    swaps = []
    for k in range(1, rows_axis):
        other = lax.rem(row_no + k, rows_axis)
        for n, (src, dst) in enumerate(
            ((bathymetry, resting.at[own_rows]), (fields.at[other], state.at[:, own_rows]))
        ):
            copy = pltpu.make_async_remote_copy(
                src_ref=src, dst_ref=dst,
                send_sem=swap_send.at[2 * k + n], recv_sem=swap_recv.at[2 * k + n],
                device_id=(group, other), device_id_type=MESH,
            )
            copy.start()
            swaps.append(copy)
    own_fields.wait()
    own_depth.wait()
    for copy in swaps:
        copy.wait()

    count = dealt.shape[1]
    lane = lax.broadcasted_iota(jnp.int32, (SUBLANES, LANES), 1)
    for col in range(cols):
        here = pl.ds(col * LANES, LANES)
        for kind in range(3):
            stage[kind, col] = state[kind, :, here]
        stage[3, col] = resting[:, here].astype(jnp.float32) / 100.0
        for k in range(count):
            every = pl.ds(k, SUBLANES, stride=count)
            for kind in range(3):
                dealt[kind, k, :, here] = stage[kind, col, every]
            deep[k, :, here] = stage[3, col, every]

    own_lists.wait()
    steps = STEPS * CYCLES
    members = sources.shape[0]
    share = -(-members // steps)

    def compose(m):
        source = m
        for cycle_no in reversed(range(lists.shape[1])):
            for section_no in reversed(range(lists.shape[0])):
                source = lists[section_no, cycle_no, source]
        sources[m] = source

    chunk_cols = cols // CHUNKS

    def forecast(q):
        first = q * chunk_cols
        follows = lane < LANES // 2
        for col in range(chunk_cols + 1):
            here = pl.ds(col * LANES, LANES)
            after = pl.ds((first + col) % cols * LANES, LANES)
            before = pl.ds((first - 1) % cols * LANES, LANES)

            def taken(ref, k, col=col, after=after, before=before):
                if col < chunk_cols:
                    return ref[k, :, after]
                return jnp.where(follows, ref[k, :, after], ref[k, :, before])

            for k in range(count):
                height, east, north = [taken(dealt.at[kind], k) for kind in range(3)]
                rest = taken(deep, k)
                work[0, k, :, here] = height
                work[1, k, :, here] = east
                work[2, k, :, here] = north
                depth[k, :, here] = rest
                flux[k, :, here] = (rest + height) * east

        def step(i, carry):
            if q == 0:
                for n in range(share):
                    compose(jnp.minimum(i * share + n, members - 1))
            for col in range(chunk_cols + 1):
                advance(work, flux, depth, middle, flux_mid, None, time_step, col, lane)
            for col in range(chunk_cols + 1):
                advance(middle, flux_mid, depth, work, flux, work, 0.5 * time_step, col, lane)
            return carry

        lax.fori_loop(0, steps, step, 0)
        for col in range(chunk_cols):
            here = pl.ds(col * LANES, LANES)
            for k in range(count):
                for kind in range(3):
                    sent[q][kind, col, pl.ds(k, SUBLANES, stride=count)] = work[kind, k, :, here]

    def core_of(i):
        return i % rows_axis

    def spread_copy(i, j):
        src = sent[i].at[
            :,
            j // count,
            pl.ds(pl.multiple_of(lax.rem(j, count) * SUBLANES, SUBLANES), SUBLANES),
        ]
        return src, pltpu.make_async_remote_copy(
            src_ref=src, dst_ref=held[i].at[me],
            send_sem=spread_send.at[i, j], recv_sem=spread_recv.at[i],
            device_id=(j, core_of(i)), device_id_type=MESH,
        )

    half = members_axis // 2
    side, seat = group // half, lax.rem(group, half)
    far, near = (1 - side) * half, side * half

    def send_all(copy, own_is_local, own_dst, own_sem):
        copy(far + seat)[1].start()

        def start(k, carry):
            there = lax.rem(seat + k, half)
            copy(far + there)[1].start()
            copy(near + there)[1].start()
            return carry

        lax.fori_loop(1, half, start, 0)
        src, remote = copy(group)

        @pl.when(own_is_local)
        def _():
            pltpu.make_async_copy(src, own_dst, own_sem).start()

        @pl.when(jnp.logical_not(own_is_local))
        def _():
            remote.start()

    def end_all(copy, own_is_local):
        def end(k, carry):
            copy(lax.rem(group + k, members_axis))[1].wait_send()
            return carry

        lax.fori_loop(1, members_axis, end, 0)

        @pl.when(jnp.logical_not(own_is_local))
        def _():
            copy(group)[1].wait_send()

    my_row = lax.rem(group, count) * SUBLANES
    home = my_row // tile_rows

    def place(i):
        return out.at[
            :,
            :,
            pl.ds(pl.multiple_of(lax.rem(my_row, tile_rows), SUBLANES), SUBLANES),
            pl.ds(
                pl.multiple_of((i * chunk_cols + group // count) * LANES, LANES),
                LANES,
            ),
        ]

    def back_copy(i, other):
        src = picked[i].at[pl.ds(other * local, local)]
        return src, pltpu.make_async_remote_copy(
            src_ref=src, dst_ref=place(i),
            send_sem=back_send.at[i, other], recv_sem=back_recv.at[i],
            device_id=(other, home), device_id_type=MESH,
        )

    for q in range(CHUNKS):
        forecast(q)
        send_all(
            functools.partial(spread_copy, q),
            row_no == core_of(q), held[q].at[me], spread_recv.at[q],
        )

    for i in range(CHUNKS):

        @pl.when(row_no == core_of(i))
        def _(i=i):
            pltpu.make_async_copy(held[i], held[i], spread_recv.at[i]).wait()
            for m in range(members):
                picked[i][m] = held[i][sources[m]]
            send_all(
                functools.partial(back_copy, i), row_no == home, place(i), back_recv.at[i]
            )

    for i in range(CHUNKS):
        end_all(functools.partial(spread_copy, i), row_no == core_of(i))

        @pl.when(row_no == core_of(i))
        def _(i=i):
            end_all(functools.partial(back_copy, i), row_no == home)

    for i in range(CHUNKS):
        landed = out.at[:, :, :, pl.ds(i * chunk_cols * LANES, chunk_cols * LANES)]
        pltpu.make_async_copy(landed, landed, back_recv.at[i]).wait()


def fast_body(members_axis, rows_axis, fields, bathymetry, copy_lists):
    local, kinds, tile_rows, width = fields.shape
    rows = tile_rows * rows_axis
    count = rows // SUBLANES
    chunk_width = width // CHUNKS + LANES
    members = members_axis * local
    f32 = jnp.float32
    dma = pltpu.SemaphoreType.DMA
    return pl.pallas_call(
        functools.partial(kernel, members_axis, rows_axis),
        out_shape=jax.ShapeDtypeStruct(fields.shape, f32),
        in_specs=[
            pl.BlockSpec(memory_space=pltpu.HBM),
            pl.BlockSpec(memory_space=pltpu.HBM),
            pl.BlockSpec(memory_space=pltpu.HBM),
        ],
        out_specs=pl.BlockSpec(memory_space=pltpu.HBM),
        scratch_shapes=[
            pltpu.VMEM((kinds, rows, width), f32),
            pltpu.VMEM((kinds + 1, width // LANES, rows, LANES), f32),
            pltpu.VMEM((kinds, count, SUBLANES, width), f32),
            pltpu.VMEM((count, SUBLANES, width), f32),
            pltpu.VMEM((kinds, count, SUBLANES, chunk_width), f32),
            pltpu.VMEM((kinds, count, SUBLANES, chunk_width), f32),
            pltpu.VMEM((count, SUBLANES, chunk_width), f32),
            pltpu.VMEM((count, SUBLANES, chunk_width), f32),
            pltpu.VMEM((rows, width), jnp.int32),
            pltpu.VMEM((count, SUBLANES, chunk_width), f32),
            [pltpu.VMEM((kinds, width // LANES // CHUNKS, rows, LANES), f32)] * CHUNKS,
            [pltpu.VMEM((members, kinds, SUBLANES, LANES), f32)] * CHUNKS,
            [pltpu.VMEM((members, kinds, SUBLANES, LANES), f32)] * CHUNKS,
            pltpu.SMEM((copy_lists.shape[1], copy_lists.shape[0], copy_lists.shape[2]), jnp.int32),
            pltpu.SMEM((members,), jnp.int32),
            dma((3,)),
            dma((2 * rows_axis,)),
            dma((2 * rows_axis,)),
            dma((CHUNKS, members_axis)),
            dma((CHUNKS,)),
            dma((CHUNKS, members_axis)),
            dma((CHUNKS,)),
        ],
        compiler_params=pltpu.CompilerParams(
            collective_id=0, has_side_effects=True
        ),
    )(fields, bathymetry, jnp.swapaxes(copy_lists, 0, 1))


def solution(mesh):
    members_axis, rows_axis = mesh.shape["member"], mesh.shape["row"]
    placed = (P("member", None, "row", None), P("row", None), P())

    def body(fields, bathymetry, copy_lists):
        local, _, tile_rows, width = fields.shape
        chunk_cols = width // (LANES * CHUNKS)
        row_tiles = tile_rows * rows_axis // SUBLANES
        fits = (
            local == rows_axis
            and width % (LANES * CHUNKS) == 0
            and tile_rows % SUBLANES == 0
            and members_axis % 2 == 0
            and members_axis == row_tiles * chunk_cols
            and 2 * STEPS * CYCLES <= LANES // 2
        )
        if fits:
            return fast_body(members_axis, rows_axis, fields, bathymetry, copy_lists)
        return general_body(fields, bathymetry, copy_lists)

    return jax.shard_map(
        body, mesh=mesh, in_specs=placed, out_specs=P("member", None, "row", None), check_vma=False
    )
```
